256 devices in a mesh: px: 16 (over y_hi, z), py: 16 (over y_lo, x, core).
Axes of the slice: x: 4, y: 4 (y_hi: 2, y_lo: 2; y = y_hi * 2 + y_lo), z: 8, core: 2. Of those that a mesh axis runs over, the one named last changes fastest.
Arguments:
- field: bfloat16 [2, 64, 64, 4096], P(None, 'px', 'py'), may hold values from -6 to 6
- cotangent: bfloat16 [2, 64, 64, 4096], P(None, 'px', 'py'), may hold values from -6 to 6
- taps: bfloat16 [3, 64, 64, 64], replicated, may hold values from -1 to 1.5, as said below
Outputs:
- mapped: bfloat16 [2, 64, 64, 4096], P(None, 'px', 'py')
- grad_field: bfloat16 [2, 64, 64, 4096], P(None, 'px', 'py')
- grad_taps: float32 [3, 64, 64, 64], P(None, 'px', 'py')
The draws below stay inside these ranges and needn't reach their ends.
Inputs may be any that keep to these rules, and one draw needn't show every extreme that they name: Every diagonal entry taps[a, 0, c, c] lies between 1 and 1.5, and every diagonal entry taps[a, t, c, c] with t >= 1 has magnitude at most 0.4 / 64.
All inputs are finite; a program needn't handle non-finite values.
Results may differ from the reference program's by a relative error of at most 0.018.
Values may be sent and summed in bfloat16 or wider, within the bound.
A program may use at most 64 MiB of HBM per device.

```python
import math
import jax
import jax.numpy as jnp
from jax import lax

N = 64
C = 64
B = 2


def draw_taps(key, part):
    key_spread, key_leading, key_trailing = jax.random.split(key, 3)
    tap_shape = (3, N, C, C)
    spread_part = jax.random.truncated_normal(key_spread, -4.0, 4.0, tap_shape, jnp.float32) * (0.15 / math.sqrt(N))
    leading = jax.random.uniform(key_leading, (3, 1, C), jnp.float32, 1.0, 1.5)
    trailing = jax.random.uniform(key_trailing, (3, N, C), jnp.float32, -0.39 / N, 0.39 / N)
    anchor_row = (jnp.arange(N) == 0)[None, :, None]
    diag_vals = jnp.where(anchor_row, leading, trailing)
    eye_mat = jnp.eye(C, dtype=jnp.float32)
    return (spread_part * (1.0 - eye_mat) + diag_vals[..., None] * eye_mat).astype(jnp.bfloat16)


def level_of(own_key, extent, cuts, least, high):
    def one(axis_at, blocks):
        heights = jax.random.uniform(jax.random.fold_in(jax.random.fold_in(own_key, 6), axis_at), (blocks,), jnp.float32, least / len(cuts), high / len(cuts))
        return jnp.repeat(jnp.exp(heights), extent[axis_at] // blocks).reshape((-1,) + (1,) * (len(extent) - axis_at - 1))

    loudness = one(*cuts[0])
    for cut in cuts[1:]:
        loudness = loudness * one(*cut)
    return loudness


def scatter_about(rng, extent, scale, most, pieces=(), kind=jnp.bfloat16):
    gain = level_of(rng, extent, pieces, -0.22, 0.18) if pieces else 1.0
    drawn = jax.random.normal(rng, extent, jnp.float32) * scale * gain
    return jnp.minimum(jnp.maximum(drawn, -most), most).astype(kind)


def setup_inputs(seed: int = 0) -> dict:
    keys = jax.random.split(jax.random.key(seed), 4)
    field = scatter_about(keys[0], (B, N, N, N * C), 1.0, 6.0, ((1, 16), (2, 16)))
    cotangent = scatter_about(keys[1], (B, N, N, N * C), 1.0, 6.0, ((1, 16), (2, 16)))
    taps = draw_taps(jax.random.fold_in(keys[3], 71), 0)
    return dict(field=field, cotangent=cotangent, taps=taps)


def dft_tables(row_ids, col_ids, length):
    product = row_ids[:, None] * col_ids[None, :] % length
    angle = product.astype(jnp.float32) * (2.0 * math.pi / length)
    return (jnp.cos(angle), jnp.sin(angle))

def along(values, table, position):
    letters = 'abcdef'[:values.ndim]
    target = letters[:position] + 'k' + letters[position + 1:]
    return jnp.einsum(letters + ',k' + letters[position] + '->' + target, values.astype(jnp.float32), table.astype(jnp.float32))

def section(values, position, cos_b, sin_b, turn_sign, factor):
    direct = along(values, cos_b, position)
    crossed = along(values, sin_b, position)
    half = values.shape[-1] // 2
    turned = jnp.concatenate([crossed[..., half:], -crossed[..., :half]], -1)
    return ((direct + turn_sign * turned) * factor).astype(jnp.bfloat16)

def z_forward(values, cos_b, sin_b):
    direct = along(values, cos_b, 3)
    crossed = along(values, sin_b, 3)
    return jnp.concatenate([direct, -crossed], -1).astype(jnp.bfloat16)

def z_inverse(values, cos_b, sin_b, factor):
    half = values.shape[-1] // 2
    real_part = along(values[..., :half], cos_b, 3)
    imag_part = along(values[..., half:], sin_b, 3)
    return ((real_part - imag_part) * factor).astype(jnp.bfloat16)

def spectra(taps_axis, cos_b, sin_b):
    taps_f = taps_axis.astype(jnp.float32)
    real_w = jnp.einsum('kt,toi->koi', cos_b.astype(jnp.float32), taps_f)
    imag_w = -jnp.einsum('kt,toi->koi', sin_b.astype(jnp.float32), taps_f)
    upper = jnp.concatenate([real_w, -imag_w], 2)
    lower = jnp.concatenate([imag_w, real_w], 2)
    return jnp.concatenate([upper, lower], 1).astype(jnp.bfloat16)

def push(values, matrix, position):
    letters = 'abcde'
    return jnp.einsum(letters + ',' + letters[position] + 'fe->abcdf', values.astype(jnp.float32), matrix.astype(jnp.float32)).astype(jnp.bfloat16)

def pull(values, matrix, position):
    letters = 'abcde'
    return jnp.einsum(letters + ',' + letters[position] + 'ef->abcdf', values.astype(jnp.float32), matrix.astype(jnp.float32)).astype(jnp.bfloat16)

def outer(left, right, position):
    letters = 'abcde'
    return jnp.einsum('abcde,abcdf->' + letters[position] + 'ef', left.astype(jnp.float32), right.astype(jnp.float32))

def tap_terms(spectral, cos_f, sin_f, split_t, split_o):
    width = spectral.shape[1] // 2
    count = spectral.shape[0]
    real_g = spectral[:, :width, :width] + spectral[:, width:, width:]
    imag_g = spectral[:, :width, width:] - spectral[:, width:, :width]
    cos_r = cos_f.reshape(count, split_t, -1)
    sin_r = sin_f.reshape(count, split_t, -1)
    real_r = real_g.reshape(count, split_o, -1, width)
    imag_r = imag_g.reshape(count, split_o, -1, width)
    highest = lax.Precision.HIGHEST
    return jnp.einsum('kpu,kqvi->pquvi', cos_r, real_r, precision=highest) + jnp.einsum('kpu,kqvi->pquvi', sin_r, imag_r, precision=highest)

def log_terms(taps, row_ids, col_ids, length):
    highest = lax.Precision.HIGHEST
    diag_w = jnp.diagonal(taps.astype(jnp.float32), axis1=2, axis2=3)
    cos_full, sin_full = dft_tables(row_ids, row_ids, length)
    real_z = jnp.einsum('kt,atc->akc', cos_full, diag_w, precision=highest)
    imag_z = -jnp.einsum('kt,atc->akc', sin_full, diag_w, precision=highest)
    modulus = real_z * real_z + imag_z * imag_z
    cos_cols, sin_cols = dft_tables(row_ids, col_ids, length)
    summed = jnp.einsum('kt,akc->atc', cos_cols, real_z / modulus, precision=highest) - jnp.einsum('kt,akc->atc', sin_cols, imag_z / modulus, precision=highest)
    return summed / math.sqrt(length)

def reference(field, cotangent, taps):
    all_ids = jnp.arange(N, dtype=jnp.int32)
    cos_f, sin_f = dft_tables(all_ids, all_ids, N)
    cos_b = cos_f.astype(jnp.bfloat16)
    sin_b = sin_f.astype(jnp.bfloat16)

    def forward_three(values):
        spectral = z_forward(values.reshape(B, N, N, N, C), cos_b, sin_b)
        spectral = section(spectral, 2, cos_b, sin_b, 1.0, 1.0)
        return section(spectral, 1, cos_b, sin_b, 1.0, 1.0)

    def inverse_three(values):
        spatial = section(values, 1, cos_b, sin_b, -1.0, 1.0 / N)
        spatial = section(spatial, 2, cos_b, sin_b, -1.0, 1.0 / N)
        return z_inverse(spatial, cos_b, sin_b, 1.0 / N).reshape(B, N, N, N * C)
    field_hat = forward_three(field)
    cot_hat = forward_three(cotangent)
    lower_mask = jnp.tril(jnp.ones((C, C), jnp.float32))
    masked = (taps.astype(jnp.float32) * lower_mask).astype(jnp.bfloat16)
    mix_x = spectra(masked[0], cos_b, sin_b)
    mix_y = spectra(masked[1], cos_b, sin_b)
    mix_z = spectra(masked[2], cos_b, sin_b)
    first = push(field_hat, mix_z, 3)
    second = push(first, mix_y, 2)
    out_hat = push(second, mix_x, 1)
    back_two = pull(cot_hat, mix_x, 1)
    back_one = pull(back_two, mix_y, 2)
    back_hat = pull(back_one, mix_z, 3)
    grad_x_spec = outer(cot_hat, second, 1)
    grad_y_spec = outer(back_two, first, 2)
    grad_z_spec = outer(back_one, field_hat, 3)
    mapped = inverse_three(out_hat)
    grad_field = inverse_three(back_hat)
    data_scale = 1.0 / (float(N) ** 4 * math.sqrt(N))
    terms = jnp.stack([tap_terms(grad_x_spec, cos_f, sin_f, 1, 1).reshape(N, C, C), tap_terms(grad_y_spec, cos_f, sin_f, 1, 1).reshape(N, C, C), tap_terms(grad_z_spec, cos_f, sin_f, 1, 1).reshape(N, C, C)], 0) * data_scale
    log_part = log_terms(taps, all_ids, all_ids, N)
    eye_mat = jnp.eye(C, dtype=jnp.float32)
    grad_taps = lower_mask * (terms - log_part[:, :, None, :] * eye_mat)
    return (mapped, grad_field, grad_taps)
```

```python
import math

import jax
import jax.numpy as jnp
import numpy as np
from jax import lax
from jax.experimental import pallas as pl
from jax.experimental.pallas import tpu as pltpu
from jax.sharding import PartitionSpec as P

N = 64
C = 64
PARTS = 16
MESH = pl.DeviceIdType.MESH
F32 = jnp.float32
BF16 = jnp.bfloat16


def lane_sign(shape, dtype=F32):
    lane = lax.broadcasted_iota(jnp.int32, shape, len(shape) - 1)
    return jnp.where(lane < 64, 1.0, -1.0).astype(dtype)


def is_left(shape):
    return lax.broadcasted_iota(jnp.int32, shape, len(shape) - 1) < 64


def swap_halves(x):
    return pltpu.roll(x, 64, x.ndim - 1)


def fft8(xs, turn):
    root = math.sqrt(0.5)

    def turned(v):
        return swap_halves(v) * turn

    def fft4(a0, a1, a2, a3):
        e0, e1, o0, o1 = a0 + a2, a0 - a2, a1 + a3, turned(a1 - a3)
        return (e0 + o0, e1 + o1, e0 - o0, e1 - o1)

    a = [xs[j] + xs[j + 4] for j in range(4)]
    b = [xs[j] - xs[j + 4] for j in range(4)]
    b1 = (b[1] + turned(b[1])) * root
    b2 = turned(b[2])
    b3 = (turned(b[3]) - b[3]) * root
    even = fft4(*a)
    odd = fft4(b[0], b1, b2, b3)
    return [(even, odd)[k % 2][k // 2] for k in range(8)]


def swap_inner(tiles, row4):
    low = row4 < 2
    u = [None] * 4
    for l in range(2):
        u[l] = jnp.where(low, tiles[l], pltpu.roll(tiles[l + 2], 2, 0))
        u[l + 2] = jnp.where(low, pltpu.roll(tiles[l], 6, 0), tiles[l + 2])
    even = row4 % 2 == 0
    v = [None] * 4
    for l in (0, 2):
        v[l] = jnp.where(even, u[l], pltpu.roll(u[l + 1], 1, 0))
        v[l + 1] = jnp.where(even, pltpu.roll(u[l], 7, 0), u[l + 1])
    return v


def swap_pair(first, second, top):
    return (
        jnp.where(top, first, pltpu.roll(second, 4, 0)),
        jnp.where(top, pltpu.roll(first, 4, 0), second),
    )


def layer_kernel(
    field_ref,
    cot_ref,
    taps_ref,
    twc_ref,
    tws_ref,
    cs_ref,
    cosf_ref,
    sinf_ref,
    mapped_ref,
    gfield_ref,
    gtaps_ref,
    taps_v,
    fold,
    mix,
    work,
    hats,
    moves_out,
    moves_in,
    terms,
    grad_out,
    grad_in,
    last_out,
    last_in,
    diag,
    logs,
    taps_sem,
    send_sems,
    recv_sems,
    gsend_sems,
    grecv_sems,
    lsend_sems,
    lrecv_sems,
):
    px = lax.axis_index("px")
    py = lax.axis_index("py")
    same = px == py
    differ = jnp.logical_not(same)

    taps_copy = pltpu.make_async_copy(taps_ref, taps_v, taps_sem)
    taps_copy.start()

    barrier = pltpu.get_barrier_semaphore()

    def greet(i, carry):
        @pl.when(i != py)
        def _():
            pl.semaphore_signal(barrier, inc=1, device_id=(px, i), device_id_type=MESH)

        @pl.when(i != px)
        def _():
            pl.semaphore_signal(barrier, inc=1, device_id=(i, py), device_id_type=MESH)

        @pl.when(jnp.logical_or(differ, i != px))
        def _():
            pl.semaphore_signal(barrier, inc=1, device_id=(py, i), device_id_type=MESH)
            pl.semaphore_signal(barrier, inc=1, device_id=(i, px), device_id_type=MESH)

        return carry

    lax.fori_loop(0, PARTS, greet, 0)

    sgn = lane_sign((1, 128))
    left8 = is_left((8, 128))
    left16 = is_left((16, 128))
    row8 = lax.broadcasted_iota(jnp.int32, (8, 128), 0)
    row4 = row8 % 4
    top = row8 < 4

    def move_route(kind, j):
        if kind == "py":
            return (px, j), py, j == py
        if kind == "px":
            return (j, py), px, j == px
        if kind == "home":
            return (j, px), py, jnp.logical_and(same, j == px)
        return (py, j), px, jnp.logical_and(same, j == py)

    def remote(src, dst, ssem, rsem, device):
        return pltpu.make_async_remote_copy(
            src_ref=src, dst_ref=dst, send_sem=ssem, recv_sem=rsem, device_id=device, device_id_type=MESH
        )

    def start_move(kind, out_at, in_at, ssem, rsem):
        mine = py if kind in ("py", "new") else px

        def step(i, carry):
            j = lax.rem(mine + 1 + i, PARTS)
            device, slot, own = move_route(kind, j)

            @pl.when(own)
            def _():
                in_at(slot)[...] = out_at(j)[...]

            @pl.when(jnp.logical_not(own))
            def _():
                remote(out_at(j), in_at(slot), ssem.at[j], rsem.at[slot], device).start()

            return carry

        lax.fori_loop(0, PARTS, step, 0)

    def own_slot(kind, s):
        if kind == "py":
            return s == py
        if kind == "px":
            return s == px
        return jnp.logical_and(same, s == px)

    def wait_in(kind, in_at, ssem, rsem):
        def step(s, carry):
            @pl.when(jnp.logical_not(own_slot(kind, s)))
            def _():
                remote(in_at(s), in_at(s), ssem.at[s], rsem.at[s], (px, py)).wait_recv()

            return carry

        lax.fori_loop(0, PARTS, step, 0)

    def wait_out(kind, out_at, ssem, rsem):
        def step(j, carry):
            @pl.when(jnp.logical_not(own_slot(kind, j)))
            def _():
                remote(out_at(j), out_at(j), ssem.at[j], rsem.at[j], (px, py)).wait_send()

            return carry

        lax.fori_loop(0, PARTS, step, 0)

    KINDS = ("new", "py", "px", "px", "py", "home")

    def blocks(ref, m):
        return lambda j: ref.at[m, pl.ds(pl.multiple_of(j * 4, 4), 4)]

    def send(m):
        start_move(KINDS[m], blocks(moves_out, m), blocks(moves_in, m), send_sems.at[m], recv_sems.at[m])

    def receive(m):
        wait_in(KINDS[m], blocks(moves_in, m), send_sems.at[m], recv_sems.at[m])

    def unpack(ref):
        def step(j, carry):
            lanes = pl.ds(pl.multiple_of(j * 128, 128), 128)
            a0 = ref[0:16, lanes].astype(F32)
            a1 = ref[16:32, lanes].astype(F32)
            work[2 * j] = jnp.where(left16, a0, swap_halves(a1))
            work[2 * j + 1] = jnp.where(left16, swap_halves(a0), a1)
            return carry

        lax.fori_loop(0, N // 2, step, 0, unroll=4)

    def repack(load, ref):
        def step(j, carry):
            lanes = pl.ds(pl.multiple_of(j * 128, 128), 128)
            a0 = load(2 * j)
            a1 = load(2 * j + 1)
            ref[0:16, lanes] = jnp.where(left16, a0, swap_halves(a1)).astype(BF16)
            ref[16:32, lanes] = jnp.where(left16, swap_halves(a0), a1).astype(BF16)
            return carry

        lax.fori_loop(0, N // 2, step, 0, unroll=4)

    def pack_inner(m):
        def step(g, carry):
            halves = [
                swap_inner([work[4 * g + l, 8 * h : 8 * h + 8, :] for l in range(4)], row4) for h in range(2)
            ]
            for b in range(4):
                moves_out[m, 4 * g + b] = jnp.concatenate([halves[0][b], halves[1][b]], 0).astype(BF16)
            return carry

        lax.fori_loop(0, PARTS, step, 0, unroll=2)

    def pack_outer(m):
        def step(g, carry):
            out = [[None, None] for _ in range(4)]
            for h in range(2):
                for h2 in range(2):
                    rows = slice(8 * h, 8 * h + 8)
                    out[2 * h][h2], out[2 * h + 1][h2] = swap_pair(
                        work[4 * g + 2 * h2, rows, :], work[4 * g + 2 * h2 + 1, rows, :], top
                    )
            for b in range(4):
                moves_out[m, 4 * g + b] = jnp.concatenate(out[b], 0).astype(BF16)
            return carry

        lax.fori_loop(0, PARTS, step, 0, unroll=2)

    def twiddle(v, row, direction):
        cos_row = twc_ref[pl.ds(row, 1), :]
        sin_row = tws_ref[pl.ds(row, 1), :] * direction
        return v * cos_row + swap_halves(v) * sin_row

    def transform_in(load):
        def step(j, carry):
            out = fft8([load(8 * m + j) for m in range(8)], sgn)
            work[j] = out[0]
            for k1 in range(1, 8):
                work[8 * k1 + j] = twiddle(out[k1], 8 * k1 + j, 1.0)
            return carry

        lax.fori_loop(0, 8, step, 0)

    def mix_spectrum(hat, axis, push):
        contract = (((1,), (1 if push else 0,)), ((), ()))

        def step(k1, carry):
            out = fft8([work[8 * k1 + j] for j in range(8)], sgn)
            mixed = []
            for k2 in range(8):
                v = out[k2].astype(BF16)
                hats[hat, k1 + 8 * k2] = v
                mixed.append(
                    lax.dot_general(v, mix[axis, k1 + 8 * k2], contract, preferred_element_type=F32)
                )
            back = fft8(mixed, -sgn)
            for j in range(8):
                work[8 * k1 + j] = twiddle(back[j], 8 * k1 + j, -1.0)
            return carry

        lax.fori_loop(0, 8, step, 0)

    def transform_out():
        def step(j, carry):
            out = fft8([work[8 * k1 + j] for k1 in range(8)], -sgn)
            for m in range(8):
                work[8 * m + j] = out[m]
            return carry

        lax.fori_loop(0, 8, step, 0)

    def arrived(m):
        return lambda n: moves_in[m, n].astype(F32)

    def stage(load, hat, axis, push):
        transform_in(load)
        mix_spectrum(hat, axis, push)
        transform_out()

    def cs_transform(emit):
        def step(k, carry):
            even = fold[0] * cs_ref[0:1, :]
            odd = jnp.zeros((C, 128), F32)
            for t in range(1, 33):
                term = fold[t] * cs_ref[pl.ds(lax.rem(k * t, N), 1), :]
                if t % 2:
                    odd = odd + term
                else:
                    even = even + term
            emit(k, even + odd)
            emit(32 - k, (even - odd) * sgn)
            return carry

        lax.fori_loop(0, 17, step, 0)

    def make_mix(axis):
        row = lax.broadcasted_iota(jnp.int32, (C, C), 0)
        col = lax.broadcasted_iota(jnp.int32, (C, C), 1)

        def step(t, carry):
            later = lax.rem(N - t, N)
            ta = taps_v[axis, t].astype(F32)
            tb = taps_v[axis, later].astype(F32)
            diag[axis, pl.ds(t, 1), :] = jnp.sum(jnp.where(row == col, ta, 0.0), 0, keepdims=True)
            diag[axis, pl.ds(later, 1), :] = jnp.sum(jnp.where(row == col, tb, 0.0), 0, keepdims=True)
            ta = jnp.where(col <= row, ta, 0.0)
            tb = jnp.where(col <= row, tb, 0.0)
            once = jnp.logical_or(t == 0, t == 32)
            both = jnp.where(once, ta, ta + tb)
            fold[t] = jnp.concatenate([both, ta - tb], 1)
            return carry

        lax.fori_loop(0, 33, step, 0)

        def emit(k, a):
            a = a * (1.0 / N)
            flipped = swap_halves(a)
            mix[axis, k] = jnp.concatenate([a, flipped * -sgn], 0).astype(BF16)
            mix[axis, lax.rem(N - k, N)] = jnp.concatenate([a * sgn, flipped], 0).astype(BF16)

        cs_transform(emit)

    def make_logs():
        highest = lax.Precision.HIGHEST

        def dot(a, b):
            return jnp.dot(a, b, precision=highest, preferred_element_type=F32)

        cos_t, sin_t = cosf_ref[...], sinf_ref[...]
        for axis in range(3):
            d = diag[axis]
            real_z, imag_z = dot(cos_t, d), -dot(sin_t, d)
            modulus = real_z * real_z + imag_z * imag_z
            logs[axis] = (dot(cos_t, real_z / modulus) - dot(sin_t, imag_z / modulus)) * (1.0 / math.sqrt(N))

    def grad_terms(axis, cot_hat, field_hat):
        sgn_b = lane_sign((16, 128), BF16)
        contract = (((0,), (0,)), ((), ()))

        def fill(p, v, u):
            g = lax.dot_general(v, u, contract, preferred_element_type=F32)
            fold[p] = g[:C] + swap_halves(g[C:]) * sgn

        fill(0, hats[cot_hat, 0], hats[field_hat, 0])
        fill(32, hats[cot_hat, 32], hats[field_hat, 32])

        def step(p, carry):
            v = jnp.concatenate([hats[cot_hat, p], hats[cot_hat, N - p] * sgn_b], 0)
            u = jnp.concatenate([hats[field_hat, p], hats[field_hat, N - p] * sgn_b], 0)
            fill(p, v, u)
            return carry

        lax.fori_loop(1, 32, step, 0)
        scale = 1.0 / (float(N) ** 2 * math.sqrt(N))

        def emit(t, h):
            h = h * scale
            flipped = swap_halves(h)
            terms[t] = h + flipped
            terms[lax.rem(N - t, N)] = (h - flipped) * sgn

        cs_transform(emit)

        def spread(g, carry):
            for q in range(8):
                rows = slice(8 * q, 8 * q + 8)
                part = [
                    jnp.where(left8, terms[8 * g + 2 * i, rows, :], terms[8 * g + 2 * i + 1, rows, :])
                    for i in range(4)
                ]
                a0, b0 = swap_pair(part[0], part[1], top)
                a1, b1 = swap_pair(part[2], part[3], top)
                grad_out[axis, 2 * q, g] = jnp.concatenate([a0, a1], 0).astype(BF16)
                grad_out[axis, 2 * q + 1, g] = jnp.concatenate([b0, b1], 0).astype(BF16)
            return carry

        lax.fori_loop(0, 8, spread, 0)
        start_move("py", *grad_ends(axis))

    def grad_ends(axis):
        return (
            lambda j: grad_out.at[axis, j],
            lambda j: grad_in.at[axis, j],
            gsend_sems.at[axis],
            grecv_sems.at[axis],
        )

    last_ends = (lambda j: last_out.at[j], lambda j: last_in.at[j], lsend_sems, lrecv_sems)

    unpack(cot_ref)
    pack_inner(0)
    pl.semaphore_wait(barrier, jnp.where(same, 4 * PARTS - 4, 4 * PARTS - 2))
    send(0)
    taps_copy.wait()
    make_mix(2)
    unpack(field_ref)
    stage(lambda n: work[n], 0, 2, True)
    pack_inner(1)
    send(1)

    make_mix(0)
    receive(0)
    stage(arrived(0), 1, 0, False)
    pack_outer(2)
    send(2)

    make_mix(1)
    receive(1)
    stage(arrived(1), 2, 1, True)
    pack_outer(3)
    send(3)

    make_logs()
    receive(2)
    stage(arrived(2), 3, 1, False)
    pack_inner(4)
    send(4)

    receive(3)
    stage(arrived(3), 4, 0, True)
    pack_inner(5)
    send(5)
    grad_terms(1, 3, 2)
    grad_terms(0, 1, 4)

    receive(4)
    stage(arrived(4), 5, 2, False)
    repack(lambda n: work[n], gfield_ref)
    grad_terms(2, 5, 0)
    receive(5)
    repack(arrived(5), mapped_ref)

    for axis in (1, 0, 2):
        start, end, ssem, rsem = grad_ends(axis)
        wait_in("py", end, ssem, rsem)

    def add_up(g, carry):
        sums = []
        for axis in range(3):
            total = grad_in[axis, 0, g].astype(F32)
            for s in range(1, PARTS):
                total = total + grad_in[axis, s, g].astype(F32)
            sums.append(total)
        for h in range(2):
            rows = slice(8 * h, 8 * h + 8)
            parts = [s[rows] for s in sums] + [jnp.zeros((8, 128), F32)]
            last_out[2 * g + h] = jnp.concatenate(parts, 0).astype(BF16)
        return carry

    lax.fori_loop(0, 8, add_up, 0)
    start_move("px", *last_ends)
    wait_in("px", last_ends[1], lsend_sems, lrecv_sems)
    total = last_in[0].astype(F32)
    for s in range(1, PARTS):
        total = total + last_in[s].astype(F32)
    row = lax.broadcasted_iota(jnp.int32, (4, C), 0) + 4 * py
    col = lax.broadcasted_iota(jnp.int32, (4, C), 1)
    for axis in range(3):
        for t in range(4):
            rows = slice(8 * axis + 4 * (t // 2), 8 * axis + 4 * (t // 2) + 4)
            own = total[rows, 64 * (t % 2) : 64 * (t % 2) + 64]
            log_row = logs[axis, pl.ds(4 * px + t, 1), :]
            own = own - jnp.where(row == col, log_row, 0.0)
            gtaps_ref[axis, t] = jnp.where(col <= row, own, 0.0)

    for m in range(6):
        wait_out(KINDS[m], blocks(moves_out, m), send_sems.at[m], recv_sems.at[m])
    for axis in range(3):
        start, end, ssem, rsem = grad_ends(axis)
        wait_out("py", start, ssem, rsem)
    wait_out("px", last_ends[0], lsend_sems, lrecv_sems)


def tables():
    angle = np.arange(N) * (2.0 * np.pi / N)
    cos = np.round(np.cos(angle), 15)
    sin = np.round(np.sin(angle), 15)
    product = np.arange(8)[:, None] * np.arange(8)[None, :]
    flat = product.reshape(-1)
    ones = np.ones((1, 64))
    twc = np.concatenate([cos[flat][:, None] * ones] * 2, 1)
    tws = np.concatenate([sin[flat][:, None] * ones, -sin[flat][:, None] * ones], 1)
    cs = np.concatenate([cos[:, None] * ones, sin[:, None] * ones], 1)
    grid = np.arange(N)[:, None] * np.arange(N)[None, :] % N
    return [np.asarray(a, np.float32) for a in (twc, tws, cs, cos[grid], sin[grid])]


def per_device(field, cotangent, taps):
    rows = field.reshape(32, N * C)
    cot_rows = cotangent.transpose(0, 2, 1, 3).reshape(32, N * C)
    vmem = pl.BlockSpec(memory_space=pltpu.VMEM)
    dma = pltpu.SemaphoreType.DMA
    mapped, gfield, gtaps = pl.pallas_call(
        layer_kernel,
        out_shape=(
            jax.ShapeDtypeStruct((32, N * C), BF16),
            jax.ShapeDtypeStruct((32, N * C), BF16),
            jax.ShapeDtypeStruct((3, 4, 4, C), F32),
        ),
        in_specs=[vmem, vmem, pl.BlockSpec(memory_space=pl.ANY)] + [vmem] * 5,
        out_specs=(vmem, vmem, vmem),
        scratch_shapes=[
            pltpu.VMEM((3, N, C, C), BF16),
            pltpu.VMEM((33, C, 128), F32),
            pltpu.VMEM((3, N, 128, 128), BF16),
            pltpu.VMEM((N, 16, 128), F32),
            pltpu.VMEM((6, N, 16, 128), BF16),
            pltpu.VMEM((6, N, 16, 128), BF16),
            pltpu.VMEM((6, N, 16, 128), BF16),
            pltpu.VMEM((N, C, 128), F32),
            pltpu.VMEM((3, PARTS, 8, 16, 128), BF16),
            pltpu.VMEM((3, PARTS, 8, 16, 128), BF16),
            pltpu.VMEM((PARTS, 32, 128), BF16),
            pltpu.VMEM((PARTS, 32, 128), BF16),
            pltpu.VMEM((3, N, C), F32),
            pltpu.VMEM((3, N, C), F32),
            dma(()),
            dma((6, PARTS)),
            dma((6, PARTS)),
            dma((3, PARTS)),
            dma((3, PARTS)),
            dma((PARTS,)),
            dma((PARTS,)),
        ],
        compiler_params=pltpu.CompilerParams(
            collective_id=0, has_side_effects=True, vmem_limit_bytes=48 * 1024 * 1024
        ),
        name="flow_layer",
    )(rows, cot_rows, taps, *[jnp.asarray(t) for t in tables()])
    mapped = mapped.reshape(2, 4, 4, N * C).transpose(0, 2, 1, 3)
    return (mapped, gfield.reshape(2, 4, 4, N * C), gtaps)


def solution(mesh):
    return jax.shard_map(
        per_device,
        mesh=mesh,
        in_specs=(P(None, "px", "py", None), P(None, "px", "py", None), P()),
        out_specs=(P(None, "px", "py", None), P(None, "px", "py", None), P(None, "px", "py", None)),
        check_vma=False,
    )
```

```python
import math

import jax
import jax.numpy as jnp
from jax import lax
from jax.experimental import pallas as pl
from jax.experimental.pallas import tpu as pltpu
from jax.sharding import PartitionSpec as P

N = 64
C = 64
PARTS = 16
MESH = pl.DeviceIdType.MESH
F32 = jnp.float32
BF16 = jnp.bfloat16


def swap_halves(x):
    return pltpu.roll(x, 64, x.ndim - 1)


def add(a, b):
    return (a[0] + b[0], a[1] + b[1])


def sub(a, b):
    return (a[0] - b[0], a[1] - b[1])


def add_turned(a, b, forward):
    if forward:
        return (a[0] + b[1], a[1] - b[0])
    return (a[0] - b[1], a[1] + b[0])


def fft8(xs, forward):
    root = math.sqrt(0.5)

    def finish(e0, e1, c, d):
        o0, o1 = add(c, d), sub(c, d)
        return (add(e0, o0), add_turned(e1, o1, forward), sub(e0, o0), add_turned(e1, o1, not forward))

    a = [add(xs[j], xs[j + 4]) for j in range(4)]
    b = [sub(xs[j], xs[j + 4]) for j in range(4)]
    b1 = add_turned(b[1], b[1], forward)
    b3 = add_turned(b[3], b[3], not forward)
    b1 = (b1[0] * root, b1[1] * root)
    b3 = (b3[0] * -root, b3[1] * -root)
    even = finish(add(a[0], a[2]), sub(a[0], a[2]), a[1], a[3])
    odd = finish(add_turned(b[0], b[2], forward), add_turned(b[0], b[2], not forward), b1, b3)
    return [(even, odd)[k % 2][k // 2] for k in range(8)]


def swap_inner(tiles, row4):
    low = row4 < 2
    u = [None] * 4
    for l in range(2):
        u[l] = jnp.where(low, tiles[l], pltpu.roll(tiles[l + 2], 2, 0))
        u[l + 2] = jnp.where(low, pltpu.roll(tiles[l], 6, 0), tiles[l + 2])
    even = row4 % 2 == 0
    v = [None] * 4
    for l in (0, 2):
        v[l] = jnp.where(even, u[l], pltpu.roll(u[l + 1], 1, 0))
        v[l + 1] = jnp.where(even, pltpu.roll(u[l], 7, 0), u[l + 1])
    return v


def swap_pair(first, second, top):
    return (
        jnp.where(top, first, pltpu.roll(second, 4, 0)),
        jnp.where(top, pltpu.roll(first, 4, 0), second),
    )


def swap_lanes(first, second, left):
    return (
        jnp.where(left, first, swap_halves(second)),
        jnp.where(left, swap_halves(first), second),
    )


def swap_outer(tiles, top, left):
    u0, u1 = swap_pair(tiles[0], tiles[1], top)
    u2, u3 = swap_pair(tiles[2], tiles[3], top)
    v0, v2 = swap_lanes(u0, u2, left)
    v1, v3 = swap_lanes(u1, u3, left)
    return [v0, v1, v2, v3]


def layer_kernel(
    field_ref,
    cot_ref,
    taps_ref,
    mapped_ref,
    gfield_ref,
    gtaps_ref,
    taps_v,
    tw_cos,
    tw_sin,
    tw_both,
    fold,
    mix,
    work,
    cot_hats,
    field_hats,
    moves_out,
    moves_in,
    terms,
    grad_out,
    grad_in,
    last_out,
    last_in,
    diag,
    logs,
    taps_sem,
    send_sems,
    recv_sems,
    gsend_sems,
    grecv_sems,
    lsend_sems,
    lrecv_sems,
):
    px = lax.axis_index("px")
    py = lax.axis_index("py")
    same = px == py
    differ = jnp.logical_not(same)

    barrier = pltpu.get_barrier_semaphore()

    def greet(i, carry):
        @pl.when(i != px)
        def _():
            pl.semaphore_signal(barrier, inc=1, device_id=(i, py), device_id_type=MESH)

        @pl.when(i != py)
        def _():
            pl.semaphore_signal(barrier, inc=1, device_id=(px, i), device_id_type=MESH)

        @pl.when(jnp.logical_or(differ, i != py))
        def _():
            pl.semaphore_signal(barrier, inc=1, device_id=(py, i), device_id_type=MESH)

        return carry

    lax.fori_loop(0, PARTS, greet, 0)

    taps_copy = pltpu.make_async_copy(taps_ref, taps_v, taps_sem)
    taps_copy.start()

    left = lax.broadcasted_iota(jnp.int32, (8, 128), 1) < 64
    sgn = jnp.where(left, 1.0, -1.0).astype(F32)
    row8 = lax.broadcasted_iota(jnp.int32, (8, 128), 0)
    row4 = row8 % 4
    top = row8 < 4

    def make_tables():
        angle = lax.broadcasted_iota(jnp.int32, (N, 128), 0).astype(F32) * (2.0 * math.pi / N)
        cos, sin = jnp.cos(angle), jnp.sin(angle)
        for r in range(N):
            c = jnp.broadcast_to(cos[r : r + 1, :], (8, 128))
            s = jnp.broadcast_to(sin[r : r + 1, :], (8, 128))
            tw_cos[r] = c
            tw_sin[r] = s
            tw_both[r] = jnp.where(left, c, s)

    def move_route(kind, j):
        if kind == "py":
            return (px, j), py, j == py
        if kind == "px":
            return (j, py), px, j == px
        return (j, px), py, jnp.logical_and(same, j == px)

    def own_slot(kind, s):
        if kind == "py":
            return s == py
        if kind == "px":
            return s == px
        return jnp.logical_and(same, s == px)

    def remote(src, dst, ssem, rsem, device):
        return pltpu.make_async_remote_copy(
            src_ref=src, dst_ref=dst, send_sem=ssem, recv_sem=rsem, device_id=device, device_id_type=MESH
        )

    def start_move(kind, out_at, in_at, ssem, rsem):
        mine = py if kind == "py" else px

        def step(i, carry):
            j = lax.rem(mine + 1 + i, PARTS)
            device, slot, own = move_route(kind, j)

            @pl.when(own)
            def _():
                in_at(slot)[...] = out_at(j)[...]

            @pl.when(jnp.logical_not(own))
            def _():
                remote(out_at(j), in_at(slot), ssem.at[j], rsem.at[slot], device).start()

            return carry

        lax.fori_loop(0, PARTS, step, 0)

    def wait_in_slot(kind, in_at, ssem, rsem, s):
        @pl.when(jnp.logical_not(own_slot(kind, s)))
        def _():
            remote(in_at(s), in_at(s), ssem.at[s], rsem.at[s], (px, py)).wait_recv()

    def wait_in(kind, in_at, ssem, rsem):
        def step(s, carry):
            wait_in_slot(kind, in_at, ssem, rsem, s)
            return carry

        lax.fori_loop(0, PARTS, step, 0)

    def wait_out(kind, out_at, ssem, rsem):
        def step(j, carry):
            @pl.when(jnp.logical_not(own_slot(kind, j)))
            def _():
                remote(out_at(j), out_at(j), ssem.at[j], rsem.at[j], (px, py)).wait_send()

            return carry

        lax.fori_loop(0, PARTS, step, 0)

    KINDS = ("px", "turn", "py", "py", "py", "px", "px")

    def blocks(ref, m):
        return lambda j: ref.at[m, pl.ds(pl.multiple_of(j * 4, 4), 4)]

    def leaving(m):
        return blocks(moves_in, 4) if m == 5 else blocks(moves_out, m)

    def send(m):
        start_move(KINDS[m], leaving(m), blocks(moves_in, m), send_sems.at[m], recv_sems.at[m])

    def receive(m):
        wait_in(KINDS[m], blocks(moves_in, m), send_sems.at[m], recv_sems.at[m])

    def forward():
        def step(i, carry):
            j = lax.rem(py + PARTS - i, PARTS)
            wait_in_slot("py", blocks(moves_in, 4), send_sems.at[4], recv_sems.at[4], j)
            device, slot, own = move_route("px", j)
            source, target = leaving(5)(j), blocks(moves_in, 5)(slot)

            @pl.when(own)
            def _():
                target[...] = source[...]

            @pl.when(jnp.logical_not(own))
            def _():
                remote(source, target, send_sems.at[5, j], recv_sems.at[5, slot], device).start()

            return carry

        lax.fori_loop(0, PARTS, step, 0)

    def unpack(ref):
        def step(i, carry):
            for u in range(2):
                j = 2 * i + u
                lanes = pl.ds(pl.multiple_of(j * 128, 128), 128)
                for box in range(2):
                    both = ref[16 * box : 16 * box + 16, lanes].astype(F32)
                    even, odd = swap_lanes(both[:8], both[8:], left)
                    work[2 * j, 8 * box : 8 * box + 8, :] = even
                    work[2 * j + 1, 8 * box : 8 * box + 8, :] = odd
            return carry

        lax.fori_loop(0, N // 4, step, 0)

    def repack(load, ref):
        def step(i, carry):
            for u in range(2):
                j = 2 * i + u
                lanes = pl.ds(pl.multiple_of(j * 128, 128), 128)
                t0, t1 = load(2 * j), load(2 * j + 1)
                for box in range(2):
                    rows = slice(8 * box, 8 * box + 8)
                    lo, hi = swap_lanes(t0[rows], t1[rows], left)
                    ref[16 * box : 16 * box + 16, lanes] = jnp.concatenate([lo, hi], 0).astype(BF16)
            return carry

        lax.fori_loop(0, N // 4, step, 0)

    def pack(m, inner):
        def step(i, carry):
            for u in range(2):
                g = 2 * i + u
                parts = []
                for box in range(2):
                    tiles = [work[4 * g + l, 8 * box : 8 * box + 8, :] for l in range(4)]
                    parts.append(swap_inner(tiles, row4) if inner else swap_outer(tiles, top, left))
                for b in range(4):
                    moves_out[m, 4 * g + b] = jnp.concatenate([parts[0][b], parts[1][b]], 0).astype(BF16)
            return carry

        lax.fori_loop(0, PARTS // 2, step, 0)

    def split(tile):
        return (tile[:8], tile[8:])

    def put(n, v):
        work[n, 0:8, :] = v[0]
        work[n, 8:16, :] = v[1]

    def twiddle(v, row, forward):
        c, s = tw_cos[row], tw_sin[row]
        if forward:
            return (v[0] * c + v[1] * s, v[1] * c - v[0] * s)
        return (v[0] * c - v[1] * s, v[1] * c + v[0] * s)

    def transform_in(load):
        def step(i, carry):
            js = (2 * i, 2 * i + 1)
            loaded = [[split(load(8 * m + j)) for m in range(8)] for j in js]
            for j, xs in zip(js, loaded):
                out = fft8(xs, True)
                put(j, out[0])
                for k1 in range(1, 8):
                    put(8 * k1 + j, twiddle(out[k1], k1 * j, True))
            return carry

        lax.fori_loop(0, 4, step, 0)

    def mix_spectrum(hats, hat, axis, push):
        def step(i, carry):
            k1s = (2 * i, 2 * i + 1)
            spectra = [fft8([split(work[8 * k1 + j]) for j in range(8)], True) for k1 in k1s]
            mixed = []
            for k1, out in zip(k1s, spectra):
                row = []
                for k2 in range(8):
                    k = k1 + 8 * k2
                    conj = k2 >= 4
                    re, im = out[k2]
                    im = -im if conj else im
                    weights = mix[axis, N - k if conj else k]
                    upright = jnp.concatenate([re, im], 0).astype(BF16)
                    if push:
                        turned = jnp.concatenate([im, -re], 0).astype(BF16)
                        v = jnp.concatenate([upright, turned], 1)
                        hats[hat, k] = v
                        y = lax.dot_general(v, weights, (((1,), (1,)), ((), ())), preferred_element_type=F32)
                        re, im = y[:8], y[8:]
                    else:
                        hats[hat, k] = upright
                        y = jnp.dot(upright, weights, preferred_element_type=F32)
                        re, im = y[:8, :128] - y[8:, 128:], y[8:, :128] + y[:8, 128:]
                    row.append((re, -im if conj else im))
                mixed.append(row)
            for k1, row in zip(k1s, mixed):
                back = fft8(row, False)
                for j in range(8):
                    put(8 * k1 + j, twiddle(back[j], k1 * j, False))
            return carry

        lax.fori_loop(0, 4, step, 0)

    def transform_out():
        def step(i, carry):
            js = (2 * i, 2 * i + 1)
            loaded = [[split(work[8 * k1 + j]) for k1 in range(8)] for j in js]
            for j, xs in zip(js, loaded):
                out = fft8(xs, False)
                for m in range(8):
                    put(8 * m + j, out[m])
            return carry

        lax.fori_loop(0, 4, step, 0)

    def arrived(m):
        return lambda n: moves_in[m, n].astype(F32)

    def stage(load, hats, hat, axis, push):
        transform_in(load)
        mix_spectrum(hats, hat, axis, push)
        transform_out()

    def cs_transform(emit):
        def step(k, carry):
            sums = [None] * 4

            def gather(which, term):
                sums[which] = term if sums[which] is None else sums[which] + term

            for t in range(33):
                f = fold[t]
                if t % 2 == 0:
                    gather(t % 4 // 2, f * tw_both[lax.rem(k * t, N)])
                else:
                    gather(2, f * tw_both[lax.rem(k * t, N)])
                    gather(3, f * tw_both[lax.rem((16 - k) * t, N)])
            near = sums[0] + sums[1]
            far = (sums[0] - sums[1]) * sgn
            emit(k, near + sums[2])
            emit(32 - k, (near - sums[2]) * sgn)
            emit(16 - k, far + sums[3])
            emit(16 + k, (far - sums[3]) * sgn)
            return carry

        lax.fori_loop(0, 9, step, 0)

    def make_mix(axis):
        row = lax.broadcasted_iota(jnp.int32, (C, C), 0)
        col = lax.broadcasted_iota(jnp.int32, (C, C), 1)

        def step(i, carry):
            for u in range(3):
                t = 3 * i + u
                later = lax.rem(N - t, N)
                ta = jnp.where(col <= row, taps_v[axis, t].astype(F32), 0.0)
                tb = jnp.where(col <= row, taps_v[axis, later].astype(F32), 0.0)
                once = jnp.logical_or(t == 0, t == 32)
                both = jnp.where(once, ta, ta + tb)
                fold[t] = jnp.concatenate([both, ta - tb], 1).reshape(8, 8, 128)
            return carry

        lax.fori_loop(0, 11, step, 0)

        def emit(k, a):
            a = a * (1.0 / N)
            flipped = swap_halves(a)
            zero = jnp.zeros_like(a)
            rows = jnp.concatenate(
                [
                    jnp.concatenate([jnp.where(left, a, zero), jnp.where(left, flipped, zero)], 2),
                    jnp.concatenate([jnp.where(left, zero, flipped), jnp.where(left, zero, a)], 2),
                ],
                0,
            )
            mix[axis, k] = rows.reshape(128, 256).astype(BF16)

        cs_transform(emit)

    def make_diag():
        row = lax.broadcasted_iota(jnp.int32, (C, C), 0)
        col = lax.broadcasted_iota(jnp.int32, (C, C), 1)
        for axis in range(3):

            def step(i, carry):
                for u in range(4):
                    t = 4 * i + u
                    ta = jnp.where(row == col, taps_v[axis, t].astype(F32), 0.0)
                    diag[axis, pl.ds(t, 1), :] = jnp.sum(ta, 0, keepdims=True)
                return carry

            lax.fori_loop(0, N // 4, step, 0)

    def make_logs():
        highest = lax.Precision.HIGHEST

        def dot(a, b):
            return jnp.dot(a, b, precision=highest, preferred_element_type=F32)

        turns = lax.broadcasted_iota(jnp.int32, (N, N), 0) * lax.broadcasted_iota(jnp.int32, (N, N), 1) % N
        angle = turns.astype(F32) * (2.0 * math.pi / N)
        cos_t, sin_t = jnp.cos(angle), jnp.sin(angle)
        for axis in range(3):
            d = diag[axis]
            real_z, imag_z = dot(cos_t, d), -dot(sin_t, d)
            modulus = real_z * real_z + imag_z * imag_z
            logs[axis] = (dot(cos_t, real_z / modulus) - dot(sin_t, imag_z / modulus)) * (1.0 / math.sqrt(N))

    def grad_terms(axis, cot_hat, field_hat):
        contract = (((0,), (0,)), ((), ()))

        def fill(ps):
            for p, v, u in ps:
                g = lax.dot_general(v, u, contract, preferred_element_type=F32).reshape(2, 8, 8, 256)
                upper_a, upper_b = g[0, :, :, :128], g[0, :, :, 128:]
                lower_a, lower_b = g[1, :, :, :128], g[1, :, :, 128:]
                fold[p] = jnp.where(left, upper_a, lower_b) + swap_halves(jnp.where(left, upper_b, lower_a))

        def pair(p):
            return (
                p,
                jnp.concatenate([cot_hats[cot_hat, p], cot_hats[cot_hat, N - p]], 0),
                jnp.concatenate([field_hats[field_hat, p], field_hats[field_hat, N - p]], 0),
            )

        fill([(p, cot_hats[cot_hat, p], field_hats[field_hat, p]) for p in (0, 32)] + [pair(31)])

        def step(i, carry):
            fill([pair(1 + 3 * i + u) for u in range(3)])
            return carry

        lax.fori_loop(0, 10, step, 0)
        scale = 1.0 / (float(N) ** 2 * math.sqrt(N))

        def emit(t, h):
            h = h * scale
            flipped = swap_halves(h)
            terms[t] = h + flipped
            terms[lax.rem(N - t, N)] = (h - flipped) * sgn

        cs_transform(emit)

        def spread(g, carry):
            for q in range(8):
                part = [jnp.where(left, terms[8 * g + 2 * i, q], terms[8 * g + 2 * i + 1, q]) for i in range(4)]
                a0, b0 = swap_pair(part[0], part[1], top)
                a1, b1 = swap_pair(part[2], part[3], top)
                grad_out[axis, 2 * q, g] = jnp.concatenate([a0, a1], 0).astype(BF16)
                grad_out[axis, 2 * q + 1, g] = jnp.concatenate([b0, b1], 0).astype(BF16)
            return carry

        lax.fori_loop(0, 8, spread, 0)
        start_move("py", *grad_ends(axis))

    def grad_ends(axis):
        return (
            lambda j: grad_out.at[axis, j],
            lambda j: grad_in.at[axis, j],
            gsend_sems.at[axis],
            grecv_sems.at[axis],
        )

    last_ends = (lambda j: last_out.at[j], lambda j: last_in.at[j], lsend_sems, lrecv_sems)

    unpack(cot_ref)
    pack(0, True)
    make_tables()
    pl.semaphore_wait(barrier, jnp.where(same, 3 * PARTS - 3, 3 * PARTS - 2))
    send(0)
    taps_copy.wait()
    make_mix(2)
    unpack(field_ref)
    stage(lambda n: work[n], field_hats, 0, 2, True)
    pack(3, True)
    send(3)

    make_mix(0)
    receive(0)
    stage(arrived(0), cot_hats, 0, 0, False)
    pack(1, False)
    send(1)

    make_mix(1)
    receive(3)
    stage(arrived(3), field_hats, 1, 1, True)
    pack(4, False)
    send(4)

    make_diag()
    forward()
    receive(1)
    stage(arrived(1), cot_hats, 1, 1, False)
    pack(2, True)
    send(2)
    grad_terms(1, 1, 1)

    receive(5)
    stage(arrived(5), field_hats, 2, 0, True)
    pack(6, True)
    send(6)
    receive(2)
    transform_in(arrived(2))
    mix_spectrum(cot_hats, 2, 2, False)
    grad_terms(2, 2, 0)
    grad_terms(0, 0, 2)
    transform_out()
    repack(lambda n: work[n], gfield_ref)
    make_logs()
    receive(6)
    repack(arrived(6), mapped_ref)

    for axis in (1, 2, 0):
        start, end, ssem, rsem = grad_ends(axis)
        wait_in("py", end, ssem, rsem)

    def add_up(g, carry):
        sums = []
        for axis in range(3):
            total = grad_in[axis, 0, g].astype(F32)
            for s in range(1, PARTS):
                total = total + grad_in[axis, s, g].astype(F32)
            sums.append(total)
        for h in range(2):
            rows = slice(8 * h, 8 * h + 8)
            parts = [s[rows] for s in sums] + [jnp.zeros((8, 128), F32)]
            last_out[2 * g + h] = jnp.concatenate(parts, 0).astype(BF16)
        return carry

    lax.fori_loop(0, 8, add_up, 0)
    start_move("px", *last_ends)
    for m in range(7):
        wait_out(KINDS[m], leaving(m), send_sems.at[m], recv_sems.at[m])
    for axis in range(3):
        start, end, ssem, rsem = grad_ends(axis)
        wait_out("py", start, ssem, rsem)
    wait_in("px", last_ends[1], lsend_sems, lrecv_sems)
    total = last_in[0].astype(F32)
    for s in range(1, PARTS):
        total = total + last_in[s].astype(F32)
    row = lax.broadcasted_iota(jnp.int32, (4, C), 0) + 4 * py
    col = lax.broadcasted_iota(jnp.int32, (4, C), 1)
    for axis in range(3):
        for t in range(4):
            rows = slice(8 * axis + 4 * (t // 2), 8 * axis + 4 * (t // 2) + 4)
            own = total[rows, 64 * (t % 2) : 64 * (t % 2) + 64]
            log_row = logs[axis, pl.ds(4 * px + t, 1), :]
            own = own - jnp.where(row == col, log_row, 0.0)
            gtaps_ref[axis, t] = jnp.where(col <= row, own, 0.0)
    wait_out("px", last_ends[0], lsend_sems, lrecv_sems)


def per_device(field, cotangent, taps):
    rows = field.reshape(32, N * C)
    cot_rows = cotangent.transpose(0, 2, 1, 3).reshape(32, N * C)
    vmem = pl.BlockSpec(memory_space=pltpu.VMEM)
    dma = pltpu.SemaphoreType.DMA
    mapped, gfield, gtaps = pl.pallas_call(
        layer_kernel,
        out_shape=(
            jax.ShapeDtypeStruct((32, N * C), BF16),
            jax.ShapeDtypeStruct((32, N * C), BF16),
            jax.ShapeDtypeStruct((3, 4, 4, C), F32),
        ),
        in_specs=[vmem, vmem, pl.BlockSpec(memory_space=pl.ANY)],
        out_specs=(vmem, vmem, vmem),
        scratch_shapes=[
            pltpu.VMEM((3, N, C, C), BF16),
            pltpu.VMEM((N, 8, 128), F32),
            pltpu.VMEM((N, 8, 128), F32),
            pltpu.VMEM((N, 8, 128), F32),
            pltpu.VMEM((33, 8, 8, 128), F32),
            pltpu.VMEM((3, 33, 128, 256), BF16),
            pltpu.VMEM((N, 16, 128), F32),
            pltpu.VMEM((3, N, 16, 128), BF16),
            pltpu.VMEM((3, N, 16, 256), BF16),
            pltpu.VMEM((7, N, 16, 128), BF16),
            pltpu.VMEM((7, N, 16, 128), BF16),
            pltpu.VMEM((N, 8, 8, 128), F32),
            pltpu.VMEM((3, PARTS, 8, 16, 128), BF16),
            pltpu.VMEM((3, PARTS, 8, 16, 128), BF16),
            pltpu.VMEM((PARTS, 32, 128), BF16),
            pltpu.VMEM((PARTS, 32, 128), BF16),
            pltpu.VMEM((3, N, C), F32),
            pltpu.VMEM((3, N, C), F32),
            dma(()),
            dma((7, PARTS)),
            dma((7, PARTS)),
            dma((3, PARTS)),
            dma((3, PARTS)),
            dma((PARTS,)),
            dma((PARTS,)),
        ],
        compiler_params=pltpu.CompilerParams(
            collective_id=0, has_side_effects=True, vmem_limit_bytes=60 * 1024 * 1024
        ),
        name="flow_layer",
    )(rows, cot_rows, taps)
    mapped = mapped.reshape(2, 4, 4, N * C).transpose(0, 2, 1, 3)
    return (mapped, gfield.reshape(2, 4, 4, N * C), gtaps)


def solution(mesh):
    return jax.shard_map(
        per_device,
        mesh=mesh,
        in_specs=(P(None, "px", "py", None), P(None, "px", "py", None), P()),
        out_specs=(P(None, "px", "py", None), P(None, "px", "py", None), P(None, "px", "py", None)),
        check_vma=False,
    )
```

```python
import math

import jax
import jax.numpy as jnp
from jax import lax
from jax.experimental import pallas as pl
from jax.experimental.pallas import tpu as pltpu
from jax.sharding import PartitionSpec as P

N = 64
C = 64
PARTS = 16
PAD = 40
STEP = 72
MESH = pl.DeviceIdType.MESH
F32 = jnp.float32
BF16 = jnp.bfloat16


def swap_halves(x):
    return pltpu.roll(x, 64, x.ndim - 1)


def add(a, b):
    return (a[0] + b[0], a[1] + b[1])


def sub(a, b):
    return (a[0] - b[0], a[1] - b[1])


def add_turned(a, b, forward):
    if forward:
        return (a[0] + b[1], a[1] - b[0])
    return (a[0] - b[1], a[1] + b[0])


def fft8(xs, forward):
    root = math.sqrt(0.5)

    def finish(e0, e1, c, d):
        o0, o1 = add(c, d), sub(c, d)
        return (add(e0, o0), add_turned(e1, o1, forward), sub(e0, o0), add_turned(e1, o1, not forward))

    a = [add(xs[j], xs[j + 4]) for j in range(4)]
    b = [sub(xs[j], xs[j + 4]) for j in range(4)]
    b1 = add_turned(b[1], b[1], forward)
    b3 = add_turned(b[3], b[3], not forward)
    b1 = (b1[0] * root, b1[1] * root)
    b3 = (b3[0] * -root, b3[1] * -root)
    even = finish(add(a[0], a[2]), sub(a[0], a[2]), a[1], a[3])
    odd = finish(add_turned(b[0], b[2], forward), add_turned(b[0], b[2], not forward), b1, b3)
    return [(even, odd)[k % 2][k // 2] for k in range(8)]


def swap_inner(tiles, row4):
    low = row4 < 2
    u = [None] * 4
    for l in range(2):
        u[l] = jnp.where(low, tiles[l], pltpu.roll(tiles[l + 2], 2, 0))
        u[l + 2] = jnp.where(low, pltpu.roll(tiles[l], 6, 0), tiles[l + 2])
    even = row4 % 2 == 0
    v = [None] * 4
    for l in (0, 2):
        v[l] = jnp.where(even, u[l], pltpu.roll(u[l + 1], 1, 0))
        v[l + 1] = jnp.where(even, pltpu.roll(u[l], 7, 0), u[l + 1])
    return v


def swap_pair(first, second, top):
    return (
        jnp.where(top, first, pltpu.roll(second, 4, 0)),
        jnp.where(top, pltpu.roll(first, 4, 0), second),
    )


def swap_lanes(first, second, left):
    return (
        jnp.where(left, first, swap_halves(second)),
        jnp.where(left, swap_halves(first), second),
    )


def swap_outer(tiles, top, left):
    u0, u1 = swap_pair(tiles[0], tiles[1], top)
    u2, u3 = swap_pair(tiles[2], tiles[3], top)
    v0, v2 = swap_lanes(u0, u2, left)
    v1, v3 = swap_lanes(u1, u3, left)
    return [v0, v1, v2, v3]


def layer_kernel(
    field_ref,
    cot_ref,
    taps_ref,
    mapped_ref,
    gfield_ref,
    gtaps_ref,
    field_v,
    cot_v,
    mapped_v,
    gfield_v,
    taps_v,
    tw_cos,
    tw_sin,
    mix_table,
    grad_table,
    wide,
    spec,
    mix,
    work,
    cot_hats,
    field_hats,
    moves_out,
    moves_in,
    grad_out,
    grad_in,
    last_rows,
    last_out,
    last_in,
    last_sum,
    diag,
    logs,
    io_sems,
    send_sems,
    recv_sems,
    gsend_sems,
    grecv_sems,
    lsend_sems,
    lrecv_sems,
):
    px = lax.axis_index("px")
    py = lax.axis_index("py")
    same = px == py
    differ = jnp.logical_not(same)

    cot_copy = pltpu.make_async_copy(cot_ref, cot_v, io_sems.at[0])
    taps_copy = pltpu.make_async_copy(taps_ref, taps_v, io_sems.at[1])
    field_copy = pltpu.make_async_copy(field_ref, field_v, io_sems.at[2])
    gfield_copy = pltpu.make_async_copy(gfield_v, gfield_ref, io_sems.at[3])
    mapped_copy = pltpu.make_async_copy(mapped_v, mapped_ref, io_sems.at[4])
    cot_copy.start()
    taps_copy.start()
    field_copy.start()

    barrier = pltpu.get_barrier_semaphore()

    def greet(i, carry):
        @pl.when(i != px)
        def _():
            pl.semaphore_signal(barrier, inc=1, device_id=(i, py), device_id_type=MESH)

        @pl.when(i != py)
        def _():
            pl.semaphore_signal(barrier, inc=1, device_id=(px, i), device_id_type=MESH)

        @pl.when(jnp.logical_or(differ, i != py))
        def _():
            pl.semaphore_signal(barrier, inc=1, device_id=(py, i), device_id_type=MESH)

        return carry

    lax.fori_loop(0, PARTS, greet, 0)

    left = lax.broadcasted_iota(jnp.int32, (8, 128), 1) < 64
    left_n = lax.broadcasted_iota(jnp.int32, (N, 128), 1) < 64
    left_p = lax.broadcasted_iota(jnp.int32, (PAD, 128), 1) < 64
    row8 = lax.broadcasted_iota(jnp.int32, (8, 128), 0)
    row4 = row8 % 4
    top = row8 < 4

    def make_tables():
        angle = lax.broadcasted_iota(jnp.int32, (N, 128), 0).astype(F32) * (2.0 * math.pi / N)
        cos, sin = jnp.cos(angle), jnp.sin(angle)
        for r in range(N):
            c = jnp.broadcast_to(cos[r : r + 1, :], (8, 128))
            s = jnp.broadcast_to(sin[r : r + 1, :], (8, 128))
            tw_cos[r] = c
            tw_sin[r] = s

        def waves(turns):
            angle = (turns & (N - 1)).astype(F32) * (2.0 * math.pi / N)
            return jnp.cos(angle), jnp.sin(angle)

        row = lax.broadcasted_iota(jnp.int32, (2 * PAD, N), 0)
        t = lax.broadcasted_iota(jnp.int32, (2 * PAD, N), 1)
        cos, sin = waves(jnp.where(row < PAD, row, row - PAD) * t)
        mix_table[...] = (jnp.where(row < PAD, cos, sin) * (1.0 / N)).astype(BF16)
        r = lax.broadcasted_iota(jnp.int32, (64, 2 * PAD), 0)
        col = lax.broadcasted_iota(jnp.int32, (64, 2 * PAD), 1)
        p = jnp.where(col < PAD, col, col - PAD)
        t = 4 * (r & 15) + 2 * ((r & 31) >> 4) + (r >> 5)
        cos, sin = waves(p * t)
        scale = 1.0 / (float(N) ** 2 * math.sqrt(N))
        value = jnp.where((r < 32) == (col < PAD), cos, sin) * scale
        grad_table[...] = jnp.where(p <= 32, value, 0.0).astype(BF16)

    def move_route(kind, j):
        if kind == "py":
            return (px, j), py, j == py
        if kind == "px":
            return (j, py), px, j == px
        return (j, px), py, jnp.logical_and(same, j == px)

    def own_slot(kind, s):
        if kind == "py":
            return s == py
        if kind == "px":
            return s == px
        return jnp.logical_and(same, s == px)

    def remote(src, dst, ssem, rsem, device):
        return pltpu.make_async_remote_copy(
            src_ref=src, dst_ref=dst, send_sem=ssem, recv_sem=rsem, device_id=device, device_id_type=MESH
        )

    def start_move(kind, out_at, in_at, ssem, rsem):
        mine = py if kind == "py" else px

        def step(i, carry):
            j = lax.rem(mine + 1 + i, PARTS)
            device, slot, own = move_route(kind, j)

            @pl.when(own)
            def _():
                in_at(slot)[...] = out_at(j)[...]

            @pl.when(jnp.logical_not(own))
            def _():
                remote(out_at(j), in_at(slot), ssem.at[j], rsem.at[slot], device).start()

            return carry

        lax.fori_loop(0, PARTS, step, 0)

    def wait_in_slot(kind, in_at, ssem, rsem, s):
        @pl.when(jnp.logical_not(own_slot(kind, s)))
        def _():
            remote(in_at(s), in_at(s), ssem.at[s], rsem.at[s], (px, py)).wait_recv()

    def wait_in(kind, in_at, ssem, rsem):
        def step(s, carry):
            wait_in_slot(kind, in_at, ssem, rsem, s)
            return carry

        lax.fori_loop(0, PARTS, step, 0)

    def wait_out(kind, out_at, ssem, rsem):
        def step(j, carry):
            @pl.when(jnp.logical_not(own_slot(kind, j)))
            def _():
                remote(out_at(j), out_at(j), ssem.at[j], rsem.at[j], (px, py)).wait_send()

            return carry

        lax.fori_loop(0, PARTS, step, 0)

    KINDS = ("px", "turn", "py", "py", "py", "px", "px")

    def blocks(ref, m):
        return lambda j: ref.at[m, pl.ds(pl.multiple_of(j * 4, 4), 4)]

    def leaving(m):
        return blocks(moves_in, 4) if m == 5 else blocks(moves_out, m)

    def send(m):
        start_move(KINDS[m], leaving(m), blocks(moves_in, m), send_sems.at[m], recv_sems.at[m])

    def receive(m):
        wait_in(KINDS[m], blocks(moves_in, m), send_sems.at[m], recv_sems.at[m])

    def forward():
        def step(i, carry):
            j = lax.rem(py + PARTS - i, PARTS)
            wait_in_slot("py", blocks(moves_in, 4), send_sems.at[4], recv_sems.at[4], j)
            device, slot, own = move_route("px", j)
            source, target = leaving(5)(j), blocks(moves_in, 5)(slot)

            @pl.when(own)
            def _():
                target[...] = source[...]

            @pl.when(jnp.logical_not(own))
            def _():
                remote(source, target, send_sems.at[5, j], recv_sems.at[5, slot], device).start()

            return carry

        lax.fori_loop(0, PARTS, step, 0)

    def flip_cells(v):
        a0, b0 = row8 // 4, row8 % 2
        v = jnp.where(a0 == b0, v, jnp.where(a0 < b0, pltpu.roll(v, 5, 0), pltpu.roll(v, 3, 0)))
        lane_bit = jnp.where(left, 0, 1)
        b1 = row8 // 2 % 2
        turned = swap_halves(v)
        return jnp.where(
            lane_bit == b1, v, jnp.where(b1 < lane_bit, pltpu.roll(turned, 6, 0), pltpu.roll(turned, 2, 0))
        )

    def unpack(ref, flip):
        def step(i, carry):
            for u in range(8):
                j = 8 * i + u
                lanes = pl.ds(pl.multiple_of(j * 128, 128), 128)
                for box in range(2):
                    rows = [ref[box, x, :, lanes].astype(F32) for x in range(4)]
                    even, odd = swap_lanes(
                        jnp.concatenate(rows[:2], 0), jnp.concatenate(rows[2:], 0), left
                    )
                    if flip:
                        even, odd = flip_cells(even), flip_cells(odd)
                    work[2 * j, 8 * box : 8 * box + 8, :] = even
                    work[2 * j + 1, 8 * box : 8 * box + 8, :] = odd
            return carry

        lax.fori_loop(0, N // 16, step, 0)

    def repack(load, ref, flip):
        def step(i, carry):
            for u in range(8):
                j = 8 * i + u
                lanes = pl.ds(pl.multiple_of(j * 128, 128), 128)
                t0, t1 = load(2 * j), load(2 * j + 1)
                for box in range(2):
                    rows = slice(8 * box, 8 * box + 8)
                    v0, v1 = t0[rows], t1[rows]
                    if flip:
                        v0, v1 = flip_cells(v0), flip_cells(v1)
                    lo, hi = swap_lanes(v0, v1, left)
                    ref[box, 0, :, lanes] = lo[:4].astype(BF16)
                    ref[box, 1, :, lanes] = lo[4:].astype(BF16)
                    ref[box, 2, :, lanes] = hi[:4].astype(BF16)
                    ref[box, 3, :, lanes] = hi[4:].astype(BF16)
            return carry

        lax.fori_loop(0, N // 16, step, 0)

    def pack(m, inner):
        def step(i, carry):
            for u in range(4):
                g = 4 * i + u
                parts = []
                for box in range(2):
                    tiles = [work[4 * g + l, 8 * box : 8 * box + 8, :] for l in range(4)]
                    parts.append(swap_inner(tiles, row4) if inner else swap_outer(tiles, top, left))
                for b in range(4):
                    moves_out[m, 4 * g + b] = jnp.concatenate([parts[0][b], parts[1][b]], 0).astype(BF16)
            return carry

        lax.fori_loop(0, PARTS // 4, step, 0)

    def split(tile):
        return (tile[:8], tile[8:])

    def put(n, v):
        work[n, 0:8, :] = v[0]
        work[n, 8:16, :] = v[1]

    def twiddle(v, row, forward):
        c, s = tw_cos[row], tw_sin[row]
        if forward:
            return (v[0] * c + v[1] * s, v[1] * c - v[0] * s)
        return (v[0] * c - v[1] * s, v[1] * c + v[0] * s)

    def transform_in(load):
        def step(i, carry):
            js = (2 * i, 2 * i + 1)
            loaded = [[split(load(8 * m + j)) for m in range(8)] for j in js]
            for j, xs in zip(js, loaded):
                out = fft8(xs, True)
                put(j, out[0])
                for k1 in range(1, 8):
                    put(8 * k1 + j, twiddle(out[k1], k1 * j, True))
            return carry

        lax.fori_loop(0, 4, step, 0)

    def mix_spectrum(hats, hat, axis, push):
        def step(i, carry):
            k1s = (2 * i, 2 * i + 1)
            spectra = [fft8([split(work[8 * k1 + j]) for j in range(8)], True) for k1 in k1s]
            mixed = []
            for k1, out in zip(k1s, spectra):
                row = []
                for k2 in range(8):
                    k = k1 + 8 * k2
                    conj = k2 >= 4
                    re, im = out[k2]
                    im = -im if conj else im
                    weights = mix[axis, N - k if conj else k]
                    upright = jnp.concatenate([re, im], 0).astype(BF16)
                    if push:
                        turned = jnp.concatenate([im, -re], 0).astype(BF16)
                        v = jnp.concatenate([upright, turned], 1)
                        hats[hat, k] = v
                        y = lax.dot_general(v, weights, (((1,), (1,)), ((), ())), preferred_element_type=F32)
                        re, im = y[:8], y[8:]
                    else:
                        hats[hat, k] = upright
                        y = jnp.dot(upright, weights, preferred_element_type=F32)
                        re, im = y[:8, :128] - y[8:, 128:], y[8:, :128] + y[:8, 128:]
                    row.append((re, -im if conj else im))
                mixed.append(row)
            for k1, row in zip(k1s, mixed):
                back = fft8(row, False)
                for j in range(8):
                    put(8 * k1 + j, twiddle(back[j], k1 * j, False))
            return carry

        lax.fori_loop(0, 4, step, 0)

    def transform_out():
        def step(i, carry):
            js = (2 * i, 2 * i + 1)
            loaded = [[split(work[8 * k1 + j]) for k1 in range(8)] for j in js]
            for j, xs in zip(js, loaded):
                out = fft8(xs, False)
                for m in range(8):
                    put(8 * m + j, out[m])
            return carry

        lax.fori_loop(0, 4, step, 0)

    def arrived(m):
        return lambda n: moves_in[m, n].astype(F32)

    def stage(load, hats, hat, axis, push):
        transform_in(load)
        mix_spectrum(hats, hat, axis, push)
        transform_out()

    def make_mix(axis):
        row = lax.broadcasted_iota(jnp.int32, (C, C), 0)
        col = lax.broadcasted_iota(jnp.int32, (C, C), 1)

        def widen(i, carry):
            for u in range(16):
                t = 16 * i + u
                ta = jnp.where(col <= row, taps_v[axis, t].astype(F32), 0.0)
                wide[pl.ds(pl.multiple_of(t * STEP, 8), C), :] = jnp.concatenate([ta, ta], 1)
            return carry

        lax.fori_loop(0, N // 16, widen, 0)

        def transform(i, carry):
            for u in range(8):
                co = 16 * i + 2 * u
                x = [wide[pl.ds(co + v, N, stride=STEP), :] for v in range(2)]
                both = jnp.concatenate(x, 1).astype(BF16)
                out = jnp.dot(mix_table[...], both, preferred_element_type=F32)
                for v in range(2):
                    lanes = slice(128 * v, 128 * v + 128)
                    spec[pl.ds(co + v, PAD, stride=STEP), :] = jnp.where(left_p, out[:PAD, lanes], out[PAD:, lanes])
            return carry

        lax.fori_loop(0, C // 16, transform, 0)

        def place(i, carry):
            for u in range(11):
                k = 11 * i + u
                a = spec[pl.ds(pl.multiple_of(k * STEP, 8), C), :]
                flipped = swap_halves(a)
                mix[axis, k] = jnp.concatenate(
                    [
                        jnp.concatenate([jnp.where(left_n, a, 0.0), jnp.where(left_n, flipped, 0.0)], 1),
                        jnp.concatenate([jnp.where(left_n, 0.0, flipped), jnp.where(left_n, 0.0, a)], 1),
                    ],
                    0,
                ).astype(BF16)
            return carry

        lax.fori_loop(0, 3, place, 0)

    def make_diag():
        row = lax.broadcasted_iota(jnp.int32, (C, C), 0)
        col = lax.broadcasted_iota(jnp.int32, (C, C), 1)
        for axis in range(3):

            def step(i, carry):
                for u in range(16):
                    t = 16 * i + u
                    ta = jnp.where(row == col, taps_v[axis, t].astype(F32), 0.0)
                    diag[axis, pl.ds(t, 1), :] = jnp.sum(ta, 0, keepdims=True)
                return carry

            lax.fori_loop(0, N // 16, step, 0)

    def make_logs():
        highest = lax.Precision.HIGHEST

        def dot(a, b):
            return jnp.dot(a, b, precision=highest, preferred_element_type=F32)

        turns = lax.broadcasted_iota(jnp.int32, (N, N), 0) * lax.broadcasted_iota(jnp.int32, (N, N), 1) % N
        angle = turns.astype(F32) * (2.0 * math.pi / N)
        cos_t, sin_t = jnp.cos(angle), jnp.sin(angle)
        for axis in range(3):
            d = diag[axis]
            real_z, imag_z = dot(cos_t, d), -dot(sin_t, d)
            modulus = real_z * real_z + imag_z * imag_z
            logs[axis] = (dot(cos_t, real_z / modulus) - dot(sin_t, imag_z / modulus)) * (1.0 / math.sqrt(N))

    def grad_terms(axis, cot_hat, field_hat):
        contract = (((0,), (0,)), ((), ()))

        def fill(ps):
            for p, v, u in ps:
                g = lax.dot_general(v, u, contract, preferred_element_type=F32)
                spec[pl.ds(pl.multiple_of(p * STEP, 8), C), :] = g

        def cot_rows(k):
            v = cot_hats[cot_hat, k]
            return [v[:, :64], v[:, 64:]]

        def field_rows(k):
            u = field_hats[field_hat, k]
            return [
                jnp.concatenate([u[:, :64], u[:, 128:192]], 1),
                jnp.concatenate([u[:, 64:128], u[:, 192:]], 1),
            ]

        def operands(p, ks):
            return (
                p,
                jnp.concatenate(sum([cot_rows(k) for k in ks], []), 0),
                jnp.concatenate(sum([field_rows(k) for k in ks], []), 0),
            )

        def pair(p):
            return operands(p, (p, N - p))

        fill([operands(0, (0,)), operands(32, (32,)), pair(31)])

        def step(i, carry):
            fill([pair(1 + 10 * i + u) for u in range(10)])
            return carry

        lax.fori_loop(0, 3, step, 0)

        def spread(i, carry):
            for u in range(8):
                part = 4 * i + u // 2
                co = 4 * part + 2 * (u % 2)
                x = [spec[pl.ds(co + v, PAD, stride=STEP), :] for v in range(2)]
                both = jnp.concatenate([jnp.concatenate([v, swap_halves(v)], 0) for v in x], 1)
                out = jnp.dot(grad_table[...], both.astype(BF16), preferred_element_type=F32)
                for v in range(2):
                    lanes = slice(128 * v, 128 * v + 128)
                    at = 32 * (2 * (u % 2) + v)
                    grad_out[axis, part, at : at + 32, :] = jnp.where(
                        left_p[:32], out[:32, lanes], out[32:, lanes]
                    ).astype(BF16)
            return carry

        lax.fori_loop(0, PARTS // 4, spread, 0)
        start_move("py", *grad_ends(axis))

    def grad_ends(axis):
        return (
            lambda j: grad_out.at[axis, j],
            lambda j: grad_in.at[axis, j],
            gsend_sems.at[axis],
            grecv_sems.at[axis],
        )

    last_ends = (lambda j: last_out.at[j], lambda j: last_in.at[j], lsend_sems, lrecv_sems)

    cot_copy.wait()
    unpack(cot_v, True)
    pack(0, True)
    pl.semaphore_wait(barrier, jnp.where(same, 3 * PARTS - 3, 3 * PARTS - 2))
    send(0)
    make_tables()
    taps_copy.wait()
    make_mix(2)
    field_copy.wait()
    unpack(field_v, False)
    stage(lambda n: work[n], field_hats, 0, 2, True)
    pack(3, True)
    send(3)

    make_mix(0)
    receive(0)
    stage(arrived(0), cot_hats, 0, 0, False)
    pack(1, False)
    send(1)

    make_mix(1)
    receive(3)
    stage(arrived(3), field_hats, 1, 1, True)
    pack(4, False)
    send(4)

    make_diag()
    forward()
    receive(1)
    stage(arrived(1), cot_hats, 1, 1, False)
    pack(2, True)
    send(2)

    grad_terms(1, 1, 1)
    receive(2)
    transform_in(arrived(2))
    mix_spectrum(cot_hats, 2, 2, False)
    grad_terms(2, 2, 0)
    transform_out()
    repack(lambda n: work[n], gfield_v, False)
    gfield_copy.start()
    receive(5)
    stage(arrived(5), field_hats, 2, 0, True)
    pack(6, True)
    send(6)

    grad_terms(0, 0, 2)

    make_logs()
    receive(6)
    repack(arrived(6), mapped_v, True)
    mapped_copy.start()

    for axis in (1, 2, 0):
        start, end, ssem, rsem = grad_ends(axis)
        wait_in("py", end, ssem, rsem)

    last_rows[...] = jnp.zeros_like(last_rows)
    for axis in range(3):

        def add_up(c, carry):
            rows = pl.ds(pl.multiple_of(32 * c, 32), 32)
            total = grad_in[axis, 0, rows, :].astype(F32)
            for s in range(1, PARTS):
                total = total + grad_in[axis, s, rows, :].astype(F32)
            for h in range(2):
                last_rows[pl.ds(8 * axis + 2 * c + h, PARTS, stride=32), :] = total[16 * h : 16 * h + 16]
            return carry

        lax.fori_loop(0, 4, add_up, 0)

    for j in range(PARTS):
        last_out[j] = last_rows[32 * j : 32 * j + 32, :].astype(BF16)
    start_move("px", *last_ends)
    for m in range(7):
        wait_out(KINDS[m], leaving(m), send_sems.at[m], recv_sems.at[m])
    for axis in range(3):
        start, end, ssem, rsem = grad_ends(axis)
        wait_out("py", start, ssem, rsem)
    wait_in("px", last_ends[1], lsend_sems, lrecv_sems)
    total = last_in[0].astype(F32)
    for s in range(1, PARTS):
        total = total + last_in[s].astype(F32)
    last_sum[...] = total
    row = lax.broadcasted_iota(jnp.int32, (4, C), 0) + 4 * py
    col = lax.broadcasted_iota(jnp.int32, (4, C), 1)
    for axis in range(3):
        for t in range(4):
            own = last_sum[pl.ds(8 * axis + t // 2, 4, stride=2), :]
            own = own[:, 64 * (t % 2) : 64 * (t % 2) + 64]
            log_row = logs[axis, pl.ds(4 * px + t, 1), :]
            own = own - jnp.where(row == col, log_row, 0.0)
            gtaps_ref[axis, t] = jnp.where(col <= row, own, 0.0)
    wait_out("px", last_ends[0], lsend_sems, lrecv_sems)
    gfield_copy.wait()
    mapped_copy.wait()


def hand_over_kernel(mapped_in, gfield_in, gtaps_in, mapped_out, gfield_out, gtaps_out, a, b, c, sems):
    legs = ((mapped_in, a, mapped_out), (gfield_in, b, gfield_out), (gtaps_in, c, gtaps_out))
    inward = [pltpu.make_async_copy(src, mid, sems.at[0, i]) for i, (src, mid, _) in enumerate(legs)]
    outward = [pltpu.make_async_copy(mid, dst, sems.at[1, i]) for i, (_, mid, dst) in enumerate(legs)]
    for copy in inward:
        copy.start()
    for first, second in zip(inward, outward):
        first.wait()
        second.start()
    for copy in outward:
        copy.wait()


def per_device(field, cotangent, taps):
    vmem = pl.BlockSpec(memory_space=pltpu.VMEM)
    anywhere = pl.BlockSpec(memory_space=pl.ANY)
    dma = pltpu.SemaphoreType.DMA
    shapes = (
        jax.ShapeDtypeStruct((2, 4, 4, N * C), BF16),
        jax.ShapeDtypeStruct((2, 4, 4, N * C), BF16),
        jax.ShapeDtypeStruct((3, 4, 4, C), F32),
    )
    results = pl.pallas_call(
        layer_kernel,
        out_shape=shapes,
        in_specs=[anywhere] * 3,
        out_specs=(anywhere, anywhere, vmem),
        scratch_shapes=[
            pltpu.VMEM((2, 4, 4, N * C), BF16),
            pltpu.VMEM((2, 4, 4, N * C), BF16),
            pltpu.VMEM((2, 4, 4, N * C), BF16),
            pltpu.VMEM((2, 4, 4, N * C), BF16),
            pltpu.VMEM((3, N, C, C), BF16),
            pltpu.VMEM((N, 8, 128), F32),
            pltpu.VMEM((N, 8, 128), F32),
            pltpu.VMEM((2 * PAD, N), BF16),
            pltpu.VMEM((64, 2 * PAD), BF16),
            pltpu.VMEM((N * STEP, 128), F32),
            pltpu.VMEM((PAD * STEP, 128), F32),
            pltpu.VMEM((3, 33, 128, 256), BF16),
            pltpu.VMEM((N, 16, 128), F32),
            pltpu.VMEM((3, N, 16, 128), BF16),
            pltpu.VMEM((3, N, 16, 256), BF16),
            pltpu.VMEM((7, N, 16, 128), BF16),
            pltpu.VMEM((7, N, 16, 128), BF16),
            pltpu.VMEM((3, PARTS, 128, 128), BF16),
            pltpu.VMEM((3, PARTS, 128, 128), BF16),
            pltpu.VMEM((PARTS * 32, 128), F32),
            pltpu.VMEM((PARTS, 32, 128), BF16),
            pltpu.VMEM((PARTS, 32, 128), BF16),
            pltpu.VMEM((32, 128), F32),
            pltpu.VMEM((3, N, C), F32),
            pltpu.VMEM((3, N, C), F32),
            dma((5,)),
            dma((7, PARTS)),
            dma((7, PARTS)),
            dma((3, PARTS)),
            dma((3, PARTS)),
            dma((PARTS,)),
            dma((PARTS,)),
        ],
        compiler_params=pltpu.CompilerParams(
            collective_id=0, has_side_effects=True, vmem_limit_bytes=60 * 1024 * 1024
        ),
        name="flow_layer",
    )(field, cotangent, taps)
    return pl.pallas_call(
        hand_over_kernel,
        out_shape=shapes,
        in_specs=[anywhere] * 3,
        out_specs=(anywhere,) * 3,
        scratch_shapes=[pltpu.VMEM(a.shape, a.dtype) for a in shapes] + [dma((2, 3))],
        compiler_params=pltpu.CompilerParams(vmem_limit_bytes=60 * 1024 * 1024),
        name="hand_over",
    )(*results)


def solution(mesh):
    return jax.shard_map(
        per_device,
        mesh=mesh,
        in_specs=(P(None, "px", "py", None), P(None, "px", "py", None), P()),
        out_specs=(P(None, "px", "py", None), P(None, "px", "py", None), P(None, "px", "py", None)),
        check_vma=False,
    )
```

```python
import math

import jax
import jax.numpy as jnp
from jax import lax
from jax.experimental import pallas as pl
from jax.experimental.pallas import tpu as pltpu
from jax.sharding import PartitionSpec as P

N = 64
C = 64
PARTS = 16
PAD = 40
STEP = 72
MESH = pl.DeviceIdType.MESH
F32 = jnp.float32
BF16 = jnp.bfloat16


def swap_halves(x):
    return pltpu.roll(x, 64, x.ndim - 1)


def add(a, b):
    return (a[0] + b[0], a[1] + b[1])


def sub(a, b):
    return (a[0] - b[0], a[1] - b[1])


def add_turned(a, b, forward):
    if forward:
        return (a[0] + b[1], a[1] - b[0])
    return (a[0] - b[1], a[1] + b[0])


def fft8(xs, forward):
    root = math.sqrt(0.5)

    def finish(e0, e1, c, d):
        o0, o1 = add(c, d), sub(c, d)
        return (add(e0, o0), add_turned(e1, o1, forward), sub(e0, o0), add_turned(e1, o1, not forward))

    a = [add(xs[j], xs[j + 4]) for j in range(4)]
    b = [sub(xs[j], xs[j + 4]) for j in range(4)]
    b1 = add_turned(b[1], b[1], forward)
    b3 = add_turned(b[3], b[3], not forward)
    b1 = (b1[0] * root, b1[1] * root)
    b3 = (b3[0] * -root, b3[1] * -root)
    even = finish(add(a[0], a[2]), sub(a[0], a[2]), a[1], a[3])
    odd = finish(add_turned(b[0], b[2], forward), add_turned(b[0], b[2], not forward), b1, b3)
    return [(even, odd)[k % 2][k // 2] for k in range(8)]


def swap_inner(tiles, row4):
    low = row4 < 2
    u = [None] * 4
    for l in range(2):
        u[l] = jnp.where(low, tiles[l], pltpu.roll(tiles[l + 2], 2, 0))
        u[l + 2] = jnp.where(low, pltpu.roll(tiles[l], 6, 0), tiles[l + 2])
    even = row4 % 2 == 0
    v = [None] * 4
    for l in (0, 2):
        v[l] = jnp.where(even, u[l], pltpu.roll(u[l + 1], 1, 0))
        v[l + 1] = jnp.where(even, pltpu.roll(u[l], 7, 0), u[l + 1])
    return v


def swap_pair(first, second, top):
    return (
        jnp.where(top, first, pltpu.roll(second, 4, 0)),
        jnp.where(top, pltpu.roll(first, 4, 0), second),
    )


def swap_lanes(first, second, left):
    return (
        jnp.where(left, first, swap_halves(second)),
        jnp.where(left, swap_halves(first), second),
    )


def swap_outer(tiles, top, left):
    u0, u1 = swap_pair(tiles[0], tiles[1], top)
    u2, u3 = swap_pair(tiles[2], tiles[3], top)
    v0, v2 = swap_lanes(u0, u2, left)
    v1, v3 = swap_lanes(u1, u3, left)
    return [v0, v1, v2, v3]


def layer_kernel(
    field_ref,
    cot_ref,
    taps_ref,
    mapped_ref,
    gfield_ref,
    gtaps_ref,
    field_v,
    cot_v,
    mapped_v,
    gfield_v,
    taps_v,
    tw_cos,
    tw_sin,
    mix_table,
    grad_table,
    wide,
    spec,
    mix,
    work_a,
    work_b,
    cot_hats,
    field_hats,
    moves_out,
    moves_in,
    grad_out,
    grad_in,
    last_rows,
    last_out,
    last_in,
    last_sum,
    diag,
    logs,
    io_sems,
    send_sems,
    recv_sems,
    gsend_sems,
    grecv_sems,
    lsend_sems,
    lrecv_sems,
):
    px = lax.axis_index("px")
    py = lax.axis_index("py")
    same = px == py
    work = work_a
    differ = jnp.logical_not(same)

    cot_copy = pltpu.make_async_copy(cot_ref, cot_v, io_sems.at[0])
    taps_copy = pltpu.make_async_copy(taps_ref, taps_v, io_sems.at[1])
    field_copy = pltpu.make_async_copy(field_ref, field_v, io_sems.at[2])
    gfield_copy = pltpu.make_async_copy(gfield_v, gfield_ref, io_sems.at[3])
    mapped_copy = pltpu.make_async_copy(mapped_v, mapped_ref, io_sems.at[4])
    cot_copy.start()
    taps_copy.start()
    field_copy.start()

    barrier = pltpu.get_barrier_semaphore()

    def greet(i, carry):
        @pl.when(i != px)
        def _():
            pl.semaphore_signal(barrier, inc=1, device_id=(i, py), device_id_type=MESH)

        @pl.when(i != py)
        def _():
            pl.semaphore_signal(barrier, inc=1, device_id=(px, i), device_id_type=MESH)

        @pl.when(jnp.logical_or(differ, i != py))
        def _():
            pl.semaphore_signal(barrier, inc=1, device_id=(py, i), device_id_type=MESH)

        return carry

    lax.fori_loop(0, PARTS, greet, 0)

    left = lax.broadcasted_iota(jnp.int32, (8, 128), 1) < 64
    left_n = lax.broadcasted_iota(jnp.int32, (N, 128), 1) < 64
    left_p = lax.broadcasted_iota(jnp.int32, (PAD, 128), 1) < 64
    row8 = lax.broadcasted_iota(jnp.int32, (8, 128), 0)
    row4 = row8 % 4
    top = row8 < 4

    def make_tables():
        angle = lax.broadcasted_iota(jnp.int32, (N, 128), 0).astype(F32) * (2.0 * math.pi / N)
        cos, sin = jnp.cos(angle), jnp.sin(angle)
        for r in range(N):
            c = jnp.broadcast_to(cos[r : r + 1, :], (8, 128))
            s = jnp.broadcast_to(sin[r : r + 1, :], (8, 128))
            tw_cos[r] = c
            tw_sin[r] = s

        def waves(turns):
            angle = (turns & (N - 1)).astype(F32) * (2.0 * math.pi / N)
            return jnp.cos(angle), jnp.sin(angle)

        row = lax.broadcasted_iota(jnp.int32, (2 * PAD, N), 0)
        t = lax.broadcasted_iota(jnp.int32, (2 * PAD, N), 1)
        cos, sin = waves(jnp.where(row < PAD, row, row - PAD) * t)
        mix_table[...] = (jnp.where(row < PAD, cos, sin) * (1.0 / N)).astype(BF16)
        r = lax.broadcasted_iota(jnp.int32, (64, 2 * PAD), 0)
        col = lax.broadcasted_iota(jnp.int32, (64, 2 * PAD), 1)
        p = jnp.where(col < PAD, col, col - PAD)
        t = 4 * (r & 15) + 2 * ((r & 31) >> 4) + (r >> 5)
        cos, sin = waves(p * t)
        scale = 1.0 / (float(N) ** 2 * math.sqrt(N))
        value = jnp.where((r < 32) == (col < PAD), cos, sin) * scale
        grad_table[...] = jnp.where(p <= 32, value, 0.0).astype(BF16)

    def move_route(kind, j):
        if kind == "py":
            return (px, j), py, j == py
        if kind == "px":
            return (j, py), px, j == px
        return (j, px), py, jnp.logical_and(same, j == px)

    def own_slot(kind, s):
        if kind == "py":
            return s == py
        if kind == "px":
            return s == px
        return jnp.logical_and(same, s == px)

    def remote(src, dst, ssem, rsem, device):
        return pltpu.make_async_remote_copy(
            src_ref=src, dst_ref=dst, send_sem=ssem, recv_sem=rsem, device_id=device, device_id_type=MESH
        )

    def start_move(kind, out_at, in_at, ssem, rsem):
        mine = py if kind == "py" else px

        def step(i, carry):
            j = lax.rem(mine + 1 + i, PARTS)
            device, slot, own = move_route(kind, j)

            @pl.when(own)
            def _():
                in_at(slot)[...] = out_at(j)[...]

            @pl.when(jnp.logical_not(own))
            def _():
                remote(out_at(j), in_at(slot), ssem.at[j], rsem.at[slot], device).start()

            return carry

        lax.fori_loop(0, PARTS, step, 0)

    def wait_in_slot(kind, in_at, ssem, rsem, s):
        @pl.when(jnp.logical_not(own_slot(kind, s)))
        def _():
            remote(in_at(s), in_at(s), ssem.at[s], rsem.at[s], (px, py)).wait_recv()

    def wait_in(kind, in_at, ssem, rsem):
        def step(s, carry):
            wait_in_slot(kind, in_at, ssem, rsem, s)
            return carry

        lax.fori_loop(0, PARTS, step, 0)

    def wait_out(kind, out_at, ssem, rsem):
        def step(j, carry):
            @pl.when(jnp.logical_not(own_slot(kind, j)))
            def _():
                remote(out_at(j), out_at(j), ssem.at[j], rsem.at[j], (px, py)).wait_send()

            return carry

        lax.fori_loop(0, PARTS, step, 0)

    KINDS = ("px", "turn", "py", "py", "py", "px", "px")

    def blocks(ref, m):
        return lambda j: ref.at[m, pl.ds(pl.multiple_of(j * 4, 4), 4)]

    def leaving(m):
        return blocks(moves_in, 4) if m == 5 else blocks(moves_out, m)

    def send(m):
        start_move(KINDS[m], leaving(m), blocks(moves_in, m), send_sems.at[m], recv_sems.at[m])

    def receive(m):
        wait_in(KINDS[m], blocks(moves_in, m), send_sems.at[m], recv_sems.at[m])

    def forward():
        def step(i, carry):
            j = lax.rem(py + PARTS - i, PARTS)
            wait_in_slot("py", blocks(moves_in, 4), send_sems.at[4], recv_sems.at[4], j)
            device, slot, own = move_route("px", j)
            source, target = leaving(5)(j), blocks(moves_in, 5)(slot)

            @pl.when(own)
            def _():
                target[...] = source[...]

            @pl.when(jnp.logical_not(own))
            def _():
                remote(source, target, send_sems.at[5, j], recv_sems.at[5, slot], device).start()

            return carry

        lax.fori_loop(0, PARTS, step, 0)

    def flip_cells(v):
        a0, b0 = row8 // 4, row8 % 2
        v = jnp.where(a0 == b0, v, jnp.where(a0 < b0, pltpu.roll(v, 5, 0), pltpu.roll(v, 3, 0)))
        lane_bit = jnp.where(left, 0, 1)
        b1 = row8 // 2 % 2
        turned = swap_halves(v)
        return jnp.where(
            lane_bit == b1, v, jnp.where(b1 < lane_bit, pltpu.roll(turned, 6, 0), pltpu.roll(turned, 2, 0))
        )

    def unpack(ref, flip):
        def step(i, carry):
            for u in range(8):
                j = 8 * i + u
                lanes = pl.ds(pl.multiple_of(j * 128, 128), 128)
                for box in range(2):
                    rows = [ref[box, x, :, lanes].astype(F32) for x in range(4)]
                    even, odd = swap_lanes(
                        jnp.concatenate(rows[:2], 0), jnp.concatenate(rows[2:], 0), left
                    )
                    if flip:
                        even, odd = flip_cells(even), flip_cells(odd)
                    work[2 * j, 8 * box : 8 * box + 8, :] = even
                    work[2 * j + 1, 8 * box : 8 * box + 8, :] = odd
            return carry

        lax.fori_loop(0, N // 16, step, 0)

    def repack(load, ref, flip):
        def step(i, carry):
            for u in range(8):
                j = 8 * i + u
                lanes = pl.ds(pl.multiple_of(j * 128, 128), 128)
                t0, t1 = load(2 * j), load(2 * j + 1)
                for box in range(2):
                    rows = slice(8 * box, 8 * box + 8)
                    v0, v1 = t0[rows], t1[rows]
                    if flip:
                        v0, v1 = flip_cells(v0), flip_cells(v1)
                    lo, hi = swap_lanes(v0, v1, left)
                    ref[box, 0, :, lanes] = lo[:4].astype(BF16)
                    ref[box, 1, :, lanes] = lo[4:].astype(BF16)
                    ref[box, 2, :, lanes] = hi[:4].astype(BF16)
                    ref[box, 3, :, lanes] = hi[4:].astype(BF16)
            return carry

        lax.fori_loop(0, N // 16, step, 0)

    def pack(m, inner):
        def step(i, carry):
            for u in range(4):
                g = 4 * i + u
                parts = []
                for box in range(2):
                    tiles = [work[4 * g + l, 8 * box : 8 * box + 8, :] for l in range(4)]
                    parts.append(swap_inner(tiles, row4) if inner else swap_outer(tiles, top, left))
                for b in range(4):
                    moves_out[m, 4 * g + b] = jnp.concatenate([parts[0][b], parts[1][b]], 0).astype(BF16)
            return carry

        lax.fori_loop(0, PARTS // 4, step, 0)

    def split(tile):
        return (tile[:8], tile[8:])

    def put(n, v):
        work[n, 0:8, :] = v[0]
        work[n, 8:16, :] = v[1]

    def twiddle(v, row, forward):
        c, s = tw_cos[row], tw_sin[row]
        if forward:
            return (v[0] * c + v[1] * s, v[1] * c - v[0] * s)
        return (v[0] * c - v[1] * s, v[1] * c + v[0] * s)

    def transform_in(load):
        def step(i, carry):
            js = (2 * i, 2 * i + 1)
            loaded = [[split(load(8 * m + j)) for m in range(8)] for j in js]
            for j, xs in zip(js, loaded):
                out = fft8(xs, True)
                put(j, out[0])
                for k1 in range(1, 8):
                    put(8 * k1 + j, twiddle(out[k1], k1 * j, True))
            return carry

        lax.fori_loop(0, 4, step, 0)

    def mix_spectrum(hats, hat, axis, push):
        def step(i, carry):
            k1s = (2 * i, 2 * i + 1)
            spectra = [fft8([split(work[8 * k1 + j]) for j in range(8)], True) for k1 in k1s]
            mixed = []
            for k1, out in zip(k1s, spectra):
                row = []
                for k2 in range(8):
                    k = k1 + 8 * k2
                    conj = k2 >= 4
                    re, im = out[k2]
                    im = -im if conj else im
                    weights = mix[axis, N - k if conj else k]
                    upright = jnp.concatenate([re, im], 0).astype(BF16)
                    if push:
                        turned = jnp.concatenate([im, -re], 0).astype(BF16)
                        v = jnp.concatenate([upright, turned], 1)
                        hats[hat, k] = v
                        y = lax.dot_general(v, weights, (((1,), (1,)), ((), ())), preferred_element_type=F32)
                        re, im = y[:8], y[8:]
                    else:
                        hats[hat, k] = upright
                        y = jnp.dot(upright, weights, preferred_element_type=F32)
                        re, im = y[:8, :128] - y[8:, 128:], y[8:, :128] + y[:8, 128:]
                    row.append((re, -im if conj else im))
                mixed.append(row)
            for k1, row in zip(k1s, mixed):
                back = fft8(row, False)
                for j in range(8):
                    put(8 * k1 + j, twiddle(back[j], k1 * j, False))
            return carry

        lax.fori_loop(0, 4, step, 0)

    def transform_out():
        def step(i, carry):
            js = (2 * i, 2 * i + 1)
            loaded = [[split(work[8 * k1 + j]) for k1 in range(8)] for j in js]
            for j, xs in zip(js, loaded):
                out = fft8(xs, False)
                for m in range(8):
                    put(8 * m + j, out[m])
            return carry

        lax.fori_loop(0, 4, step, 0)

    def arrived(m):
        return lambda n: moves_in[m, n].astype(F32)

    def stage(load, hats, hat, axis, push):
        transform_in(load)
        mix_spectrum(hats, hat, axis, push)
        transform_out()

    def make_mix(axis):
        row = lax.broadcasted_iota(jnp.int32, (C, C), 0)
        col = lax.broadcasted_iota(jnp.int32, (C, C), 1)

        def widen(i, carry):
            for u in range(16):
                t = 16 * i + u
                ta = jnp.where(col <= row, taps_v[axis, t].astype(F32), 0.0)
                wide[pl.ds(pl.multiple_of(t * STEP, 8), C), :] = jnp.concatenate([ta, ta], 1)
            return carry

        lax.fori_loop(0, N // 16, widen, 0)

        def transform(i, carry):
            for u in range(8):
                co = 16 * i + 2 * u
                x = [wide[pl.ds(co + v, N, stride=STEP), :] for v in range(2)]
                both = jnp.concatenate(x, 1).astype(BF16)
                out = jnp.dot(mix_table[...], both, preferred_element_type=F32)
                for v in range(2):
                    lanes = slice(128 * v, 128 * v + 128)
                    spec[pl.ds(co + v, PAD, stride=STEP), :] = jnp.where(left_p, out[:PAD, lanes], out[PAD:, lanes])
            return carry

        lax.fori_loop(0, C // 16, transform, 0)

        def place(i, carry):
            for u in range(11):
                k = 11 * i + u
                a = spec[pl.ds(pl.multiple_of(k * STEP, 8), C), :]
                flipped = swap_halves(a)
                mix[axis, k] = jnp.concatenate(
                    [
                        jnp.concatenate([jnp.where(left_n, a, 0.0), jnp.where(left_n, flipped, 0.0)], 1),
                        jnp.concatenate([jnp.where(left_n, 0.0, flipped), jnp.where(left_n, 0.0, a)], 1),
                    ],
                    0,
                ).astype(BF16)
            return carry

        lax.fori_loop(0, 3, place, 0)

    def make_diag():
        row = lax.broadcasted_iota(jnp.int32, (C, C), 0)
        col = lax.broadcasted_iota(jnp.int32, (C, C), 1)
        for axis in range(3):

            def step(i, carry):
                for u in range(16):
                    t = 16 * i + u
                    ta = jnp.where(row == col, taps_v[axis, t].astype(F32), 0.0)
                    diag[axis, pl.ds(t, 1), :] = jnp.sum(ta, 0, keepdims=True)
                return carry

            lax.fori_loop(0, N // 16, step, 0)

    def make_logs():
        highest = lax.Precision.HIGHEST

        def dot(a, b):
            return jnp.dot(a, b, precision=highest, preferred_element_type=F32)

        turns = lax.broadcasted_iota(jnp.int32, (N, N), 0) * lax.broadcasted_iota(jnp.int32, (N, N), 1) % N
        angle = turns.astype(F32) * (2.0 * math.pi / N)
        cos_t, sin_t = jnp.cos(angle), jnp.sin(angle)
        for axis in range(3):
            d = diag[axis]
            real_z, imag_z = dot(cos_t, d), -dot(sin_t, d)
            modulus = real_z * real_z + imag_z * imag_z
            logs[axis] = (dot(cos_t, real_z / modulus) - dot(sin_t, imag_z / modulus)) * (1.0 / math.sqrt(N))

    def grad_terms(axis, cot_hat, field_hat):
        contract = (((0,), (0,)), ((), ()))

        def fill(ps):
            for p, v, u in ps:
                g = lax.dot_general(v, u, contract, preferred_element_type=F32)
                spec[pl.ds(pl.multiple_of(p * STEP, 8), C), :] = g

        def cot_rows(k):
            v = cot_hats[cot_hat, k]
            return [v[:, :64], v[:, 64:]]

        def field_rows(k):
            u = field_hats[field_hat, k]
            return [
                jnp.concatenate([u[:, :64], u[:, 128:192]], 1),
                jnp.concatenate([u[:, 64:128], u[:, 192:]], 1),
            ]

        def operands(p, ks):
            return (
                p,
                jnp.concatenate(sum([cot_rows(k) for k in ks], []), 0),
                jnp.concatenate(sum([field_rows(k) for k in ks], []), 0),
            )

        def pair(p):
            return operands(p, (p, N - p))

        fill([operands(0, (0,)), operands(32, (32,)), pair(31)])

        def step(i, carry):
            fill([pair(1 + 10 * i + u) for u in range(10)])
            return carry

        lax.fori_loop(0, 3, step, 0)

        def spread(i, carry):
            for u in range(8):
                part = 4 * i + u // 2
                co = 4 * part + 2 * (u % 2)
                x = [spec[pl.ds(co + v, PAD, stride=STEP), :] for v in range(2)]
                both = jnp.concatenate([jnp.concatenate([v, swap_halves(v)], 0) for v in x], 1)
                out = jnp.dot(grad_table[...], both.astype(BF16), preferred_element_type=F32)
                for v in range(2):
                    lanes = slice(128 * v, 128 * v + 128)
                    at = 32 * (2 * (u % 2) + v)
                    grad_out[axis, part, at : at + 32, :] = jnp.where(
                        left_p[:32], out[:32, lanes], out[32:, lanes]
                    ).astype(BF16)
            return carry

        lax.fori_loop(0, PARTS // 4, spread, 0)
        start_move("py", *grad_ends(axis))

    def grad_ends(axis):
        return (
            lambda j: grad_out.at[axis, j],
            lambda j: grad_in.at[axis, j],
            gsend_sems.at[axis],
            grecv_sems.at[axis],
        )

    last_ends = (lambda j: last_out.at[j], lambda j: last_in.at[j], lsend_sems, lrecv_sems)

    cot_copy.wait()
    unpack(cot_v, True)
    pack(0, True)
    pl.semaphore_wait(barrier, jnp.where(same, 3 * PARTS - 3, 3 * PARTS - 2))
    send(0)
    make_tables()
    taps_copy.wait()
    make_mix(2)
    field_copy.wait()
    unpack(field_v, False)
    stage(lambda n: work[n], field_hats, 0, 2, True)
    pack(3, True)
    send(3)

    make_mix(0)
    receive(0)
    stage(arrived(0), cot_hats, 0, 0, False)
    pack(1, False)
    send(1)

    make_mix(1)
    receive(3)
    stage(arrived(3), field_hats, 1, 1, True)
    pack(4, False)
    send(4)

    make_diag()
    forward()
    receive(1)
    stage(arrived(1), cot_hats, 1, 1, False)
    pack(2, True)
    send(2)

    grad_terms(1, 1, 1)
    receive(2)
    work = work_b
    transform_in(arrived(2))
    mix_spectrum(cot_hats, 2, 2, False)
    grad_terms(2, 2, 0)
    receive(5)
    work = work_a
    stage(arrived(5), field_hats, 2, 0, True)
    pack(6, True)
    send(6)

    grad_terms(0, 0, 2)
    work = work_b
    transform_out()
    repack(lambda n: work[n], gfield_v, False)
    gfield_copy.start()

    make_logs()
    receive(6)
    repack(arrived(6), mapped_v, True)
    mapped_copy.start()

    last_rows[...] = jnp.zeros_like(last_rows)
    for axis in (1, 2, 0):
        start, end, ssem, rsem = grad_ends(axis)
        wait_in("py", end, ssem, rsem)

        def add_up(c, carry):
            rows = pl.ds(pl.multiple_of(32 * c, 32), 32)
            total = grad_in[axis, 0, rows, :].astype(F32)
            for s in range(1, PARTS):
                total = total + grad_in[axis, s, rows, :].astype(F32)
            for h in range(2):
                last_rows[pl.ds(8 * axis + 2 * c + h, PARTS, stride=32), :] = total[16 * h : 16 * h + 16]
            return carry

        lax.fori_loop(0, 4, add_up, 0)

    for j in range(PARTS):
        last_out[j] = last_rows[32 * j : 32 * j + 32, :].astype(BF16)
    start_move("px", *last_ends)
    for m in range(7):
        wait_out(KINDS[m], leaving(m), send_sems.at[m], recv_sems.at[m])
    for axis in range(3):
        start, end, ssem, rsem = grad_ends(axis)
        wait_out("py", start, ssem, rsem)
    wait_in("px", last_ends[1], lsend_sems, lrecv_sems)
    total = last_in[0].astype(F32)
    for s in range(1, PARTS):
        total = total + last_in[s].astype(F32)
    last_sum[...] = total
    row = lax.broadcasted_iota(jnp.int32, (4, C), 0) + 4 * py
    col = lax.broadcasted_iota(jnp.int32, (4, C), 1)
    for axis in range(3):
        for t in range(4):
            own = last_sum[pl.ds(8 * axis + t // 2, 4, stride=2), :]
            own = own[:, 64 * (t % 2) : 64 * (t % 2) + 64]
            log_row = logs[axis, pl.ds(4 * px + t, 1), :]
            own = own - jnp.where(row == col, log_row, 0.0)
            gtaps_ref[axis, t] = jnp.where(col <= row, own, 0.0)
    wait_out("px", last_ends[0], lsend_sems, lrecv_sems)
    gfield_copy.wait()
    mapped_copy.wait()


def hand_over_kernel(mapped_in, gfield_in, gtaps_in, mapped_out, gfield_out, gtaps_out, a, b, c, sems):
    legs = ((mapped_in, a, mapped_out), (gfield_in, b, gfield_out), (gtaps_in, c, gtaps_out))
    inward = [pltpu.make_async_copy(src, mid, sems.at[0, i]) for i, (src, mid, _) in enumerate(legs)]
    outward = [pltpu.make_async_copy(mid, dst, sems.at[1, i]) for i, (_, mid, dst) in enumerate(legs)]
    for copy in inward:
        copy.start()
    for first, second in zip(inward, outward):
        first.wait()
        second.start()
    for copy in outward:
        copy.wait()


def per_device(field, cotangent, taps):
    vmem = pl.BlockSpec(memory_space=pltpu.VMEM)
    anywhere = pl.BlockSpec(memory_space=pl.ANY)
    dma = pltpu.SemaphoreType.DMA
    shapes = (
        jax.ShapeDtypeStruct((2, 4, 4, N * C), BF16),
        jax.ShapeDtypeStruct((2, 4, 4, N * C), BF16),
        jax.ShapeDtypeStruct((3, 4, 4, C), F32),
    )
    results = pl.pallas_call(
        layer_kernel,
        out_shape=shapes,
        in_specs=[anywhere] * 3,
        out_specs=(anywhere, anywhere, vmem),
        scratch_shapes=[
            pltpu.VMEM((2, 4, 4, N * C), BF16),
            pltpu.VMEM((2, 4, 4, N * C), BF16),
            pltpu.VMEM((2, 4, 4, N * C), BF16),
            pltpu.VMEM((2, 4, 4, N * C), BF16),
            pltpu.VMEM((3, N, C, C), BF16),
            pltpu.VMEM((N, 8, 128), F32),
            pltpu.VMEM((N, 8, 128), F32),
            pltpu.VMEM((2 * PAD, N), BF16),
            pltpu.VMEM((64, 2 * PAD), BF16),
            pltpu.VMEM((N * STEP, 128), F32),
            pltpu.VMEM((PAD * STEP, 128), F32),
            pltpu.VMEM((3, 33, 128, 256), BF16),
            pltpu.VMEM((N, 16, 128), F32),
            pltpu.VMEM((N, 16, 128), F32),
            pltpu.VMEM((3, N, 16, 128), BF16),
            pltpu.VMEM((3, N, 16, 256), BF16),
            pltpu.VMEM((7, N, 16, 128), BF16),
            pltpu.VMEM((7, N, 16, 128), BF16),
            pltpu.VMEM((3, PARTS, 128, 128), BF16),
            pltpu.VMEM((3, PARTS, 128, 128), BF16),
            pltpu.VMEM((PARTS * 32, 128), F32),
            pltpu.VMEM((PARTS, 32, 128), BF16),
            pltpu.VMEM((PARTS, 32, 128), BF16),
            pltpu.VMEM((32, 128), F32),
            pltpu.VMEM((3, N, C), F32),
            pltpu.VMEM((3, N, C), F32),
            dma((5,)),
            dma((7, PARTS)),
            dma((7, PARTS)),
            dma((3, PARTS)),
            dma((3, PARTS)),
            dma((PARTS,)),
            dma((PARTS,)),
        ],
        compiler_params=pltpu.CompilerParams(
            collective_id=0, has_side_effects=True, vmem_limit_bytes=60 * 1024 * 1024
        ),
        name="flow_layer",
    )(field, cotangent, taps)
    return pl.pallas_call(
        hand_over_kernel,
        out_shape=shapes,
        in_specs=[anywhere] * 3,
        out_specs=(anywhere,) * 3,
        scratch_shapes=[pltpu.VMEM(a.shape, a.dtype) for a in shapes] + [dma((2, 3))],
        compiler_params=pltpu.CompilerParams(vmem_limit_bytes=60 * 1024 * 1024),
        name="hand_over",
    )(*results)


def solution(mesh):
    return jax.shard_map(
        per_device,
        mesh=mesh,
        in_specs=(P(None, "px", "py", None), P(None, "px", "py", None), P()),
        out_specs=(P(None, "px", "py", None), P(None, "px", "py", None), P(None, "px", "py", None)),
        check_vma=False,
    )
```

```python
import math

import jax
import jax.numpy as jnp
from jax import lax
from jax.experimental import pallas as pl
from jax.experimental.pallas import tpu as pltpu
from jax.sharding import PartitionSpec as P

N = 64
C = 64
PARTS = 16
PAD = 40
STEP = 72
MESH = pl.DeviceIdType.MESH
F32 = jnp.float32
BF16 = jnp.bfloat16


def swap_halves(x):
    return pltpu.roll(x, 64, x.ndim - 1)


def add(a, b):
    return (a[0] + b[0], a[1] + b[1])


def sub(a, b):
    return (a[0] - b[0], a[1] - b[1])


def add_turned(a, b, forward):
    if forward:
        return (a[0] + b[1], a[1] - b[0])
    return (a[0] - b[1], a[1] + b[0])


def fft8(xs, forward):
    root = math.sqrt(0.5)

    def finish(e0, e1, c, d):
        o0, o1 = add(c, d), sub(c, d)
        return (add(e0, o0), add_turned(e1, o1, forward), sub(e0, o0), add_turned(e1, o1, not forward))

    a = [add(xs[j], xs[j + 4]) for j in range(4)]
    b = [sub(xs[j], xs[j + 4]) for j in range(4)]
    b1 = add_turned(b[1], b[1], forward)
    b3 = add_turned(b[3], b[3], not forward)
    b1 = (b1[0] * root, b1[1] * root)
    b3 = (b3[0] * -root, b3[1] * -root)
    even = finish(add(a[0], a[2]), sub(a[0], a[2]), a[1], a[3])
    odd = finish(add_turned(b[0], b[2], forward), add_turned(b[0], b[2], not forward), b1, b3)
    return [(even, odd)[k % 2][k // 2] for k in range(8)]


def swap_inner(tiles, row4):
    low = row4 < 2
    u = [None] * 4
    for l in range(2):
        u[l] = jnp.where(low, tiles[l], pltpu.roll(tiles[l + 2], 2, 0))
        u[l + 2] = jnp.where(low, pltpu.roll(tiles[l], 6, 0), tiles[l + 2])
    even = row4 % 2 == 0
    v = [None] * 4
    for l in (0, 2):
        v[l] = jnp.where(even, u[l], pltpu.roll(u[l + 1], 1, 0))
        v[l + 1] = jnp.where(even, pltpu.roll(u[l], 7, 0), u[l + 1])
    return v


def swap_pair(first, second, top):
    return (
        jnp.where(top, first, pltpu.roll(second, 4, 0)),
        jnp.where(top, pltpu.roll(first, 4, 0), second),
    )


def swap_lanes(first, second, left):
    return (
        jnp.where(left, first, swap_halves(second)),
        jnp.where(left, swap_halves(first), second),
    )


def swap_outer(tiles, top, left):
    u0, u1 = swap_pair(tiles[0], tiles[1], top)
    u2, u3 = swap_pair(tiles[2], tiles[3], top)
    v0, v2 = swap_lanes(u0, u2, left)
    v1, v3 = swap_lanes(u1, u3, left)
    return [v0, v1, v2, v3]


def layer_kernel(
    field_ref,
    cot_ref,
    taps_ref,
    mapped_ref,
    gfield_ref,
    gtaps_ref,
    field_v,
    cot_v,
    mapped_v,
    gfield_v,
    taps_v,
    tw_cos,
    tw_sin,
    mix_table,
    grad_table,
    wide,
    spec,
    mix,
    work,
    cot_hats,
    field_hats,
    moves_out,
    moves_in,
    grad_out,
    grad_in,
    last_rows,
    last_out,
    last_in,
    last_sum,
    diag,
    logs,
    io_sems,
    send_sems,
    recv_sems,
    gsend_sems,
    grecv_sems,
    lsend_sems,
    lrecv_sems,
):
    px = lax.axis_index("px")
    py = lax.axis_index("py")
    same = px == py
    differ = jnp.logical_not(same)

    cot_copy = pltpu.make_async_copy(cot_ref, cot_v, io_sems.at[0])
    taps_copy = pltpu.make_async_copy(taps_ref, taps_v, io_sems.at[1])
    field_copy = pltpu.make_async_copy(field_ref, field_v, io_sems.at[2])
    gfield_copy = pltpu.make_async_copy(gfield_v, gfield_ref, io_sems.at[3])
    mapped_copy = pltpu.make_async_copy(mapped_v, mapped_ref, io_sems.at[4])
    cot_copy.start()
    taps_copy.start()
    field_copy.start()

    barrier = pltpu.get_barrier_semaphore()

    def greet(i, carry):
        @pl.when(i != px)
        def _():
            pl.semaphore_signal(barrier, inc=1, device_id=(i, py), device_id_type=MESH)

        @pl.when(i != py)
        def _():
            pl.semaphore_signal(barrier, inc=1, device_id=(px, i), device_id_type=MESH)

        @pl.when(jnp.logical_or(differ, i != py))
        def _():
            pl.semaphore_signal(barrier, inc=1, device_id=(py, i), device_id_type=MESH)

        return carry

    lax.fori_loop(0, PARTS, greet, 0)

    left = lax.broadcasted_iota(jnp.int32, (8, 128), 1) < 64
    left_n = lax.broadcasted_iota(jnp.int32, (N, 128), 1) < 64
    left_p = lax.broadcasted_iota(jnp.int32, (PAD, 128), 1) < 64
    row8 = lax.broadcasted_iota(jnp.int32, (8, 128), 0)
    row4 = row8 % 4
    top = row8 < 4

    def make_tables():
        angle = lax.broadcasted_iota(jnp.int32, (N, 128), 0).astype(F32) * (2.0 * math.pi / N)
        cos, sin = jnp.cos(angle), jnp.sin(angle)
        for r in range(N):
            c = jnp.broadcast_to(cos[r : r + 1, :], (8, 128))
            s = jnp.broadcast_to(sin[r : r + 1, :], (8, 128))
            tw_cos[r] = c
            tw_sin[r] = s

        def waves(turns):
            angle = (turns & (N - 1)).astype(F32) * (2.0 * math.pi / N)
            return jnp.cos(angle), jnp.sin(angle)

        row = lax.broadcasted_iota(jnp.int32, (2 * PAD, N), 0)
        t = lax.broadcasted_iota(jnp.int32, (2 * PAD, N), 1)
        cos, sin = waves(jnp.where(row < PAD, row, row - PAD) * t)
        mix_table[...] = (jnp.where(row < PAD, cos, sin) * (1.0 / N)).astype(BF16)
        r = lax.broadcasted_iota(jnp.int32, (64, 2 * PAD), 0)
        col = lax.broadcasted_iota(jnp.int32, (64, 2 * PAD), 1)
        p = jnp.where(col < PAD, col, col - PAD)
        t = 4 * (r & 15) + 2 * ((r & 31) >> 4) + (r >> 5)
        cos, sin = waves(p * t)
        scale = 1.0 / (float(N) ** 2 * math.sqrt(N))
        value = jnp.where((r < 32) == (col < PAD), cos, sin) * scale
        grad_table[...] = jnp.where(p <= 32, value, 0.0).astype(BF16)

    def move_route(kind, j):
        if kind == "py":
            return (px, j), py, j == py
        if kind == "px":
            return (j, py), px, j == px
        return (j, px), py, jnp.logical_and(same, j == px)

    def own_slot(kind, s):
        if kind == "py":
            return s == py
        if kind == "px":
            return s == px
        return jnp.logical_and(same, s == px)

    def remote(src, dst, ssem, rsem, device):
        return pltpu.make_async_remote_copy(
            src_ref=src, dst_ref=dst, send_sem=ssem, recv_sem=rsem, device_id=device, device_id_type=MESH
        )

    def start_move(kind, out_at, in_at, ssem, rsem):
        mine = py if kind == "py" else px

        def step(i, carry):
            j = lax.rem(mine + 1 + i, PARTS)
            device, slot, own = move_route(kind, j)

            @pl.when(own)
            def _():
                in_at(slot)[...] = out_at(j)[...]

            @pl.when(jnp.logical_not(own))
            def _():
                remote(out_at(j), in_at(slot), ssem.at[j], rsem.at[slot], device).start()

            return carry

        lax.fori_loop(0, PARTS, step, 0)

    def wait_in_slot(kind, in_at, ssem, rsem, s):
        @pl.when(jnp.logical_not(own_slot(kind, s)))
        def _():
            remote(in_at(s), in_at(s), ssem.at[s], rsem.at[s], (px, py)).wait_recv()

    def wait_in(kind, in_at, ssem, rsem):
        def step(s, carry):
            wait_in_slot(kind, in_at, ssem, rsem, s)
            return carry

        lax.fori_loop(0, PARTS, step, 0)

    def wait_out(kind, out_at, ssem, rsem):
        def step(j, carry):
            @pl.when(jnp.logical_not(own_slot(kind, j)))
            def _():
                remote(out_at(j), out_at(j), ssem.at[j], rsem.at[j], (px, py)).wait_send()

            return carry

        lax.fori_loop(0, PARTS, step, 0)

    KINDS = ("px", "turn", "py", "py", "py", "px", "px")

    def blocks(ref, m):
        return lambda j: ref.at[m, pl.ds(pl.multiple_of(j * 4, 4), 4)]

    def leaving(m):
        return blocks(moves_in, 4) if m == 5 else blocks(moves_out, m)

    def send(m):
        start_move(KINDS[m], leaving(m), blocks(moves_in, m), send_sems.at[m], recv_sems.at[m])

    def receive(m):
        wait_in(KINDS[m], blocks(moves_in, m), send_sems.at[m], recv_sems.at[m])

    def forward():
        def step(i, carry):
            j = lax.rem(py + PARTS - i, PARTS)
            wait_in_slot("py", blocks(moves_in, 4), send_sems.at[4], recv_sems.at[4], j)
            device, slot, own = move_route("px", j)
            source, target = leaving(5)(j), blocks(moves_in, 5)(slot)

            @pl.when(own)
            def _():
                target[...] = source[...]

            @pl.when(jnp.logical_not(own))
            def _():
                remote(source, target, send_sems.at[5, j], recv_sems.at[5, slot], device).start()

            return carry

        lax.fori_loop(0, PARTS, step, 0)

    def flip_cells(v):
        a0, b0 = row8 // 4, row8 % 2
        v = jnp.where(a0 == b0, v, jnp.where(a0 < b0, pltpu.roll(v, 5, 0), pltpu.roll(v, 3, 0)))
        lane_bit = jnp.where(left, 0, 1)
        b1 = row8 // 2 % 2
        turned = swap_halves(v)
        return jnp.where(
            lane_bit == b1, v, jnp.where(b1 < lane_bit, pltpu.roll(turned, 6, 0), pltpu.roll(turned, 2, 0))
        )

    def unpack(ref, flip):
        def step(i, carry):
            for u in range(8):
                j = 8 * i + u
                lanes = pl.ds(pl.multiple_of(j * 128, 128), 128)
                for box in range(2):
                    rows = [ref[box, x, :, lanes].astype(F32) for x in range(4)]
                    even, odd = swap_lanes(
                        jnp.concatenate(rows[:2], 0), jnp.concatenate(rows[2:], 0), left
                    )
                    if flip:
                        even, odd = flip_cells(even), flip_cells(odd)
                    work[2 * j, 8 * box : 8 * box + 8, :] = even
                    work[2 * j + 1, 8 * box : 8 * box + 8, :] = odd
            return carry

        lax.fori_loop(0, N // 16, step, 0)

    def repack(load, ref, flip):
        def step(i, carry):
            for u in range(8):
                j = 8 * i + u
                lanes = pl.ds(pl.multiple_of(j * 128, 128), 128)
                t0, t1 = load(2 * j), load(2 * j + 1)
                for box in range(2):
                    rows = slice(8 * box, 8 * box + 8)
                    v0, v1 = t0[rows], t1[rows]
                    if flip:
                        v0, v1 = flip_cells(v0), flip_cells(v1)
                    lo, hi = swap_lanes(v0, v1, left)
                    ref[box, 0, :, lanes] = lo[:4].astype(BF16)
                    ref[box, 1, :, lanes] = lo[4:].astype(BF16)
                    ref[box, 2, :, lanes] = hi[:4].astype(BF16)
                    ref[box, 3, :, lanes] = hi[4:].astype(BF16)
            return carry

        lax.fori_loop(0, N // 16, step, 0)

    def pack(m, inner):
        def step(i, carry):
            for u in range(4):
                g = 4 * i + u
                parts = []
                for box in range(2):
                    tiles = [work[4 * g + l, 8 * box : 8 * box + 8, :] for l in range(4)]
                    parts.append(swap_inner(tiles, row4) if inner else swap_outer(tiles, top, left))
                for b in range(4):
                    moves_out[m, 4 * g + b] = jnp.concatenate([parts[0][b], parts[1][b]], 0).astype(BF16)
            return carry

        lax.fori_loop(0, PARTS // 4, step, 0)

    def split(tile):
        return (tile[:8], tile[8:])

    def put(n, v):
        work[n, 0:8, :] = v[0]
        work[n, 8:16, :] = v[1]

    def twiddle(v, row, forward):
        c, s = tw_cos[row], tw_sin[row]
        if forward:
            return (v[0] * c + v[1] * s, v[1] * c - v[0] * s)
        return (v[0] * c - v[1] * s, v[1] * c + v[0] * s)

    def transform_in(load):
        def step(i, carry):
            js = (2 * i, 2 * i + 1)
            loaded = [[split(load(8 * m + j)) for m in range(8)] for j in js]
            for j, xs in zip(js, loaded):
                out = fft8(xs, True)
                put(j, out[0])
                for k1 in range(1, 8):
                    put(8 * k1 + j, twiddle(out[k1], k1 * j, True))
            return carry

        lax.fori_loop(0, 4, step, 0)

    def mix_spectrum(hats, hat, axis, push):
        def step(i, carry):
            k1s = (2 * i, 2 * i + 1)
            spectra = [fft8([split(work[8 * k1 + j]) for j in range(8)], True) for k1 in k1s]
            mixed = []
            for k1, out in zip(k1s, spectra):
                row = []
                for k2 in range(8):
                    k = k1 + 8 * k2
                    conj = k2 >= 4
                    re, im = out[k2]
                    im = -im if conj else im
                    weights = mix[axis, N - k if conj else k]
                    upright = jnp.concatenate([re, im], 0).astype(BF16)
                    if push:
                        turned = jnp.concatenate([im, -re], 0).astype(BF16)
                        v = jnp.concatenate([upright, turned], 1)
                        hats[hat, k] = v
                        y = lax.dot_general(v, weights, (((1,), (1,)), ((), ())), preferred_element_type=F32)
                        re, im = y[:8], y[8:]
                    else:
                        hats[hat, k] = upright
                        y = jnp.dot(upright, weights, preferred_element_type=F32)
                        re, im = y[:8, :128] - y[8:, 128:], y[8:, :128] + y[:8, 128:]
                    row.append((re, -im if conj else im))
                mixed.append(row)
            for k1, row in zip(k1s, mixed):
                back = fft8(row, False)
                for j in range(8):
                    put(8 * k1 + j, twiddle(back[j], k1 * j, False))
            return carry

        lax.fori_loop(0, 4, step, 0)

    def transform_out():
        def step(i, carry):
            js = (2 * i, 2 * i + 1)
            loaded = [[split(work[8 * k1 + j]) for k1 in range(8)] for j in js]
            for j, xs in zip(js, loaded):
                out = fft8(xs, False)
                for m in range(8):
                    put(8 * m + j, out[m])
            return carry

        lax.fori_loop(0, 4, step, 0)

    def arrived(m):
        return lambda n: moves_in[m, n].astype(F32)

    def stage(load, hats, hat, axis, push):
        transform_in(load)
        mix_spectrum(hats, hat, axis, push)
        transform_out()

    def make_mix(axis):
        row = lax.broadcasted_iota(jnp.int32, (C, C), 0)
        col = lax.broadcasted_iota(jnp.int32, (C, C), 1)

        def widen(i, carry):
            for u in range(16):
                t = 16 * i + u
                ta = jnp.where(col <= row, taps_v[axis, t].astype(F32), 0.0)
                wide[pl.ds(pl.multiple_of(t * STEP, 8), C), :] = jnp.concatenate([ta, ta], 1)
            return carry

        lax.fori_loop(0, N // 16, widen, 0)

        def transform(i, carry):
            for u in range(8):
                co = 16 * i + 2 * u
                x = [wide[pl.ds(co + v, N, stride=STEP), :] for v in range(2)]
                both = jnp.concatenate(x, 1).astype(BF16)
                out = jnp.dot(mix_table[...], both, preferred_element_type=F32)
                for v in range(2):
                    lanes = slice(128 * v, 128 * v + 128)
                    spec[pl.ds(co + v, PAD, stride=STEP), :] = jnp.where(left_p, out[:PAD, lanes], out[PAD:, lanes])
            return carry

        lax.fori_loop(0, C // 16, transform, 0)

        def place(i, carry):
            for u in range(11):
                k = 11 * i + u
                a = spec[pl.ds(pl.multiple_of(k * STEP, 8), C), :]
                flipped = swap_halves(a)
                mix[axis, k] = jnp.concatenate(
                    [
                        jnp.concatenate([jnp.where(left_n, a, 0.0), jnp.where(left_n, flipped, 0.0)], 1),
                        jnp.concatenate([jnp.where(left_n, 0.0, flipped), jnp.where(left_n, 0.0, a)], 1),
                    ],
                    0,
                ).astype(BF16)
            return carry

        lax.fori_loop(0, 3, place, 0)

    def make_diag():
        row = lax.broadcasted_iota(jnp.int32, (C, C), 0)
        col = lax.broadcasted_iota(jnp.int32, (C, C), 1)
        for axis in range(3):

            def step(i, carry):
                for u in range(16):
                    t = 16 * i + u
                    ta = jnp.where(row == col, taps_v[axis, t].astype(F32), 0.0)
                    diag[axis, pl.ds(t, 1), :] = jnp.sum(ta, 0, keepdims=True)
                return carry

            lax.fori_loop(0, N // 16, step, 0)

    def make_logs():
        highest = lax.Precision.HIGHEST

        def dot(a, b):
            return jnp.dot(a, b, precision=highest, preferred_element_type=F32)

        turns = lax.broadcasted_iota(jnp.int32, (N, N), 0) * lax.broadcasted_iota(jnp.int32, (N, N), 1) % N
        angle = turns.astype(F32) * (2.0 * math.pi / N)
        cos_t, sin_t = jnp.cos(angle), jnp.sin(angle)
        for axis in range(3):
            d = diag[axis]
            real_z, imag_z = dot(cos_t, d), -dot(sin_t, d)
            modulus = real_z * real_z + imag_z * imag_z
            logs[axis] = (dot(cos_t, real_z / modulus) - dot(sin_t, imag_z / modulus)) * (1.0 / math.sqrt(N))

    def grad_terms(axis, cot_hat, field_hat):
        contract = (((0,), (0,)), ((), ()))

        def fill(ps):
            for p, v, u in ps:
                g = lax.dot_general(v, u, contract, preferred_element_type=F32)
                spec[pl.ds(pl.multiple_of(p * STEP, 8), C), :] = g

        def cot_rows(k):
            v = cot_hats[cot_hat, k]
            return [v[:, :64], v[:, 64:]]

        def field_rows(k):
            u = field_hats[field_hat, k]
            return [
                jnp.concatenate([u[:, :64], u[:, 128:192]], 1),
                jnp.concatenate([u[:, 64:128], u[:, 192:]], 1),
            ]

        def operands(p, ks):
            return (
                p,
                jnp.concatenate(sum([cot_rows(k) for k in ks], []), 0),
                jnp.concatenate(sum([field_rows(k) for k in ks], []), 0),
            )

        def pair(p):
            return operands(p, (p, N - p))

        fill([operands(0, (0,)), operands(32, (32,)), pair(31)])

        def step(i, carry):
            fill([pair(1 + 10 * i + u) for u in range(10)])
            return carry

        lax.fori_loop(0, 3, step, 0)

        def spread(i, carry, narrow):
            for u in range(8):
                part = 4 * i + u // 2
                co = 4 * part + 2 * (u % 2)
                x = [spec[pl.ds(co + v, PAD, stride=STEP), :] for v in range(2)]
                both = jnp.concatenate([jnp.concatenate([v, swap_halves(v)], 0) for v in x], 1)
                out = jnp.dot(grad_table[...], both.astype(BF16), preferred_element_type=F32)
                a, b = [
                    jnp.where(left_p[:32], out[:32, 128 * v : 128 * v + 128], out[32:, 128 * v : 128 * v + 128])
                    for v in range(2)
                ]
                if narrow:
                    at = 32 * (u % 2)
                    grad_out[axis, part, at : at + 32, :] = jnp.where(low_half, a, pltpu.roll(b, 32, 1)).astype(BF16)
                else:
                    at = 64 * (u % 2)
                    grad_out[axis, part, at : at + 32, :] = a.astype(BF16)
                    grad_out[axis, part, at + 32 : at + 64, :] = b.astype(BF16)
            return carry

        low_half = lax.broadcasted_iota(jnp.int32, (32, 128), 1) % 64 < 32
        lax.fori_loop(0, 2, lambda i, carry: spread(i, carry, True), 0)
        lax.fori_loop(2, 4, lambda i, carry: spread(i, carry, False), 0)

        def go(i, carry):
            j = lax.rem(py + 1 + i, PARTS)
            for size, here in ((64, j < 8), (128, j >= 8)):
                start, end, ssem, rsem = grad_ends(axis, size)

                @pl.when(jnp.logical_and(here, j == py))
                def _():
                    end(py)[...] = start(j)[...]

                @pl.when(jnp.logical_and(here, j != py))
                def _():
                    remote(start(j), end(py), ssem.at[j], rsem.at[py], (px, j)).start()

            return carry

        lax.fori_loop(0, PARTS, go, 0)

    def grad_ends(axis, size):
        return (
            lambda j: grad_out.at[axis, j, pl.ds(0, size)],
            lambda j: grad_in.at[axis, j, pl.ds(0, size)],
            gsend_sems.at[axis],
            grecv_sems.at[axis],
        )

    last_ends = (lambda j: last_out.at[j], lambda j: last_in.at[j], lsend_sems, lrecv_sems)

    cot_copy.wait()
    unpack(cot_v, True)
    pack(0, True)
    pl.semaphore_wait(barrier, jnp.where(same, 3 * PARTS - 3, 3 * PARTS - 2))
    send(0)
    make_tables()
    taps_copy.wait()
    make_mix(2)
    field_copy.wait()
    unpack(field_v, False)
    stage(lambda n: work[n], field_hats, 0, 2, True)
    pack(3, True)
    send(3)

    make_mix(0)
    receive(0)
    stage(arrived(0), cot_hats, 0, 0, False)
    pack(1, False)
    send(1)

    make_mix(1)
    receive(3)
    stage(arrived(3), field_hats, 1, 1, True)
    pack(4, False)
    send(4)

    make_diag()
    forward()
    receive(1)
    stage(arrived(1), cot_hats, 1, 1, False)
    pack(2, True)
    send(2)

    grad_terms(1, 1, 1)
    receive(2)
    transform_in(arrived(2))
    mix_spectrum(cot_hats, 2, 2, False)
    grad_terms(2, 2, 0)
    transform_out()
    repack(lambda n: work[n], gfield_v, False)
    gfield_copy.start()
    receive(5)
    stage(arrived(5), field_hats, 2, 0, True)
    pack(6, True)
    send(6)

    grad_terms(0, 0, 2)

    make_logs()
    receive(6)
    repack(arrived(6), mapped_v, True)
    mapped_copy.start()

    last_rows[...] = jnp.zeros_like(last_rows)

    def collect(size):
        for axis in (1, 2, 0):
            start, end, ssem, rsem = grad_ends(axis, size)
            wait_in("py", end, ssem, rsem)

            def add_up(c, carry):
                rows = pl.ds(pl.multiple_of(32 * c, 32), 32)
                total = grad_in[axis, 0, rows, :].astype(F32)
                for s in range(1, PARTS):
                    total = total + grad_in[axis, s, rows, :].astype(F32)
                for h in range(2):
                    half = total[16 * h : 16 * h + 16]
                    if size == 64:
                        last_rows[pl.ds(8 * axis + 4 * c + h, PARTS, stride=32), :] = half
                        last_rows[pl.ds(8 * axis + 4 * c + 2 + h, PARTS, stride=32), :] = pltpu.roll(half, 96, 1)
                    else:
                        last_rows[pl.ds(8 * axis + 2 * c + h, PARTS, stride=32), :] = half
                return carry

            lax.fori_loop(0, size // 32, add_up, 0)

    @pl.when(py < 8)
    def _():
        collect(64)

    @pl.when(py >= 8)
    def _():
        collect(128)

    for j in range(PARTS):
        last_out[j] = last_rows[32 * j : 32 * j + 32, :].astype(BF16)
    start_move("px", *last_ends)
    for m in range(7):
        wait_out(KINDS[m], leaving(m), send_sems.at[m], recv_sems.at[m])
    for axis in range(3):

        def sent(j, carry):
            for size, here in ((64, j < 8), (128, j >= 8)):
                start, end, ssem, rsem = grad_ends(axis, size)

                @pl.when(jnp.logical_and(here, j != py))
                def _():
                    remote(start(j), start(j), ssem.at[j], rsem.at[j], (px, py)).wait_send()

            return carry

        lax.fori_loop(0, PARTS, sent, 0)
    wait_in("px", last_ends[1], lsend_sems, lrecv_sems)
    total = last_in[0].astype(F32)
    for s in range(1, PARTS):
        total = total + last_in[s].astype(F32)
    last_sum[...] = total
    row = lax.broadcasted_iota(jnp.int32, (4, C), 0) + 4 * py
    col = lax.broadcasted_iota(jnp.int32, (4, C), 1)
    for axis in range(3):
        for t in range(4):
            own = last_sum[pl.ds(8 * axis + t // 2, 4, stride=2), :]
            own = own[:, 64 * (t % 2) : 64 * (t % 2) + 64]
            log_row = logs[axis, pl.ds(4 * px + t, 1), :]
            own = own - jnp.where(row == col, log_row, 0.0)
            gtaps_ref[axis, t] = jnp.where(col <= row, own, 0.0)
    wait_out("px", last_ends[0], lsend_sems, lrecv_sems)
    gfield_copy.wait()
    mapped_copy.wait()


def hand_over_kernel(mapped_in, gfield_in, gtaps_in, mapped_out, gfield_out, gtaps_out, a, b, c, sems):
    legs = ((mapped_in, a, mapped_out), (gfield_in, b, gfield_out), (gtaps_in, c, gtaps_out))
    inward = [pltpu.make_async_copy(src, mid, sems.at[0, i]) for i, (src, mid, _) in enumerate(legs)]
    outward = [pltpu.make_async_copy(mid, dst, sems.at[1, i]) for i, (_, mid, dst) in enumerate(legs)]
    for copy in inward:
        copy.start()
    for first, second in zip(inward, outward):
        first.wait()
        second.start()
    for copy in outward:
        copy.wait()


def per_device(field, cotangent, taps):
    vmem = pl.BlockSpec(memory_space=pltpu.VMEM)
    anywhere = pl.BlockSpec(memory_space=pl.ANY)
    dma = pltpu.SemaphoreType.DMA
    shapes = (
        jax.ShapeDtypeStruct((2, 4, 4, N * C), BF16),
        jax.ShapeDtypeStruct((2, 4, 4, N * C), BF16),
        jax.ShapeDtypeStruct((3, 4, 4, C), F32),
    )
    results = pl.pallas_call(
        layer_kernel,
        out_shape=shapes,
        in_specs=[anywhere] * 3,
        out_specs=(anywhere, anywhere, vmem),
        scratch_shapes=[
            pltpu.VMEM((2, 4, 4, N * C), BF16),
            pltpu.VMEM((2, 4, 4, N * C), BF16),
            pltpu.VMEM((2, 4, 4, N * C), BF16),
            pltpu.VMEM((2, 4, 4, N * C), BF16),
            pltpu.VMEM((3, N, C, C), BF16),
            pltpu.VMEM((N, 8, 128), F32),
            pltpu.VMEM((N, 8, 128), F32),
            pltpu.VMEM((2 * PAD, N), BF16),
            pltpu.VMEM((64, 2 * PAD), BF16),
            pltpu.VMEM((N * STEP, 128), F32),
            pltpu.VMEM((PAD * STEP, 128), F32),
            pltpu.VMEM((3, 33, 128, 256), BF16),
            pltpu.VMEM((N, 16, 128), F32),
            pltpu.VMEM((3, N, 16, 128), BF16),
            pltpu.VMEM((3, N, 16, 256), BF16),
            pltpu.VMEM((7, N, 16, 128), BF16),
            pltpu.VMEM((7, N, 16, 128), BF16),
            pltpu.VMEM((3, PARTS, 128, 128), BF16),
            pltpu.VMEM((3, PARTS, 128, 128), BF16),
            pltpu.VMEM((PARTS * 32, 128), F32),
            pltpu.VMEM((PARTS, 32, 128), BF16),
            pltpu.VMEM((PARTS, 32, 128), BF16),
            pltpu.VMEM((32, 128), F32),
            pltpu.VMEM((3, N, C), F32),
            pltpu.VMEM((3, N, C), F32),
            dma((5,)),
            dma((7, PARTS)),
            dma((7, PARTS)),
            dma((3, PARTS)),
            dma((3, PARTS)),
            dma((PARTS,)),
            dma((PARTS,)),
        ],
        compiler_params=pltpu.CompilerParams(
            collective_id=0, has_side_effects=True, vmem_limit_bytes=60 * 1024 * 1024
        ),
        name="flow_layer",
    )(field, cotangent, taps)
    return pl.pallas_call(
        hand_over_kernel,
        out_shape=shapes,
        in_specs=[anywhere] * 3,
        out_specs=(anywhere,) * 3,
        scratch_shapes=[pltpu.VMEM(a.shape, a.dtype) for a in shapes] + [dma((2, 3))],
        compiler_params=pltpu.CompilerParams(vmem_limit_bytes=60 * 1024 * 1024),
        name="hand_over",
    )(*results)


def solution(mesh):
    return jax.shard_map(
        per_device,
        mesh=mesh,
        in_specs=(P(None, "px", "py", None), P(None, "px", "py", None), P()),
        out_specs=(P(None, "px", "py", None), P(None, "px", "py", None), P(None, "px", "py", None)),
        check_vma=False,
    )
```
